32 devices in a mesh: grp: 4 (over x, core), tp: 4 (over z), ex: 2 (over y).
Axes of the slice: x: 2, y: 2, z: 4, core: 2. Of those that a mesh axis runs over, the one named last changes fastest.
Arguments:
- tokens: bfloat16 [128, 7168], P(('grp', 'tp'), 'ex'), may hold values from -6 to 6
- expert_ids: int32 [128, 1], P(('grp', 'tp')), may hold values from 0 to 1; in each aligned block of 8 rows (0 to 7, 8 to 15, ...) at most 6 rows name the same one
- gate_levels: int32 [128, 1], P(('grp', 'tp')), may hold values from 1 to 4095
- gate_weight: bfloat16 [4, 7168, 1024], P('grp', 'ex', 'tp'), may hold values from -0.0625 to 0.0625
- up_weight: bfloat16 [4, 7168, 1024], P('grp', 'ex', 'tp'), may hold values from -0.0625 to 0.0625
- down_weight: bfloat16 [4, 1024, 7168], P('grp', 'tp', 'ex'), may hold values from -0.125 to 0.125
Outputs:
- mixed: bfloat16 [128, 7168], P(('grp', 'tp'), 'ex')
The draws below stay inside these ranges and needn't reach their ends.
Inputs may be any that keep to these rules, and one draw needn't show every extreme that they name: `expert_ids`: each row names 1 different experts. In each aligned block of 8 rows (the tokens of one index pair of grp and tp) no expert is named by more than 6 rows.
All inputs are finite; a program needn't handle non-finite values.
Results may differ from the reference program's by a relative error of at most 0.0057.
Values may be sent and summed in bfloat16 or wider, within the bound.
No kernel may reach another device: no remote copies, remote signals or barrier semaphores. Data moves between devices by JAX's collectives and lax.ppermute only.
A program may use at most 64 MiB of HBM per device.

```python
import math
import jax
import jax.numpy as jnp
import numpy as np
from jax import lax

D = 7168
H = 2048
TOK = 8
EXPERTS = 2
TOPK = 1
CAP = 6
TOKENS = 128
N_GRP = 4
N_TP = 4


def set_ends(result, key, low, high):
    index_at = [jax.random.randint(jax.random.fold_in(key, axis), (), 0, length) for axis, length in enumerate(result.shape)]
    widest = result.shape.index(max(result.shape))
    neighbour = index_at[:widest] + [(index_at[widest] + 1) % result.shape[widest]] + index_at[widest + 1:]
    return result.at[tuple(index_at)].set(low).at[tuple(neighbour)].set(high)


def shard_levels(stream_key, dims, shards, least, top_value):
    level, own = 1.0, jax.random.fold_in(stream_key, 6)
    for dim, parts in shards:
        heights = jnp.exp(jax.random.uniform(jax.random.fold_in(own, dim), (parts,), jnp.float32, least / len(shards), top_value / len(shards)))
        level = level * jnp.repeat(heights, dims[dim] // parts).reshape([-1 if axis == dim else 1 for axis in range(len(dims))])
    return level


def shared_out(stream_key, own, number, rows, amount, top, bound, skew):
    ranking = jax.random.permutation(stream_key, amount)
    heavy_load, common = portions_of(amount, rows * top, bound, skew, True), portions_of(amount, rows * top, bound, skew, False)
    places = jnp.arange(amount)

    def named(sizes, rotation):
        used = int((sizes > 0).sum())
        fixed = max(1, used // 4)
        passed = fixed + (places - fixed + rotation * (used - fixed)) % max(1, amount - fixed)
        return jnp.zeros((amount,), jnp.int32).at[ranking[jnp.where(places < fixed, places, passed)]].set(jnp.asarray(sizes, jnp.int32))

    sizes = jnp.where(number % 4 == 0, named(heavy_load, number // 4), named(common, number - number // 4 - 1))
    mixed = jax.random.permutation(jax.random.fold_in(own, 3), amount)
    source_of, sink = mixed[0:amount // 2 * 2:2], mixed[1:amount // 2 * 2:2]
    room = jnp.minimum(sizes[source_of] - 1, bound - sizes[sink]) // 2
    room = jnp.where((source_of == ranking[0]) | (sink == ranking[0]) | (sizes[sink] == 0), 0, jnp.maximum(room, 0))
    passed = jax.random.randint(jax.random.fold_in(own, 4), (amount // 2,), 0, 1 << 20) % (room + 1)
    sizes = sizes.at[source_of].add(-passed).at[sink].add(passed)
    items = jnp.searchsorted(jnp.cumsum(sizes), jnp.arange(rows * top), side="right").astype(jnp.int32)
    table = items.reshape(top, rows).T
    table = table[jax.random.permutation(jax.random.fold_in(own, 1), rows)]
    rotation = jax.random.randint(jax.random.fold_in(own, 2), (rows, 1), 0, top)
    return jnp.take_along_axis(table, (jnp.arange(top)[None, :] + rotation) % top, axis=1)


def portions_of(number_of, total, reach, lean, full):
    weights = [(1 << 20) // math.isqrt(grade ** lean) + 1 for grade in range(1, number_of + 1)]
    largest = reach if full else min(reach, max(-(-total // number_of), total * weights[0] // sum(weights)))
    least = 1 if total - largest >= number_of - 1 else 0
    holding, spare = [largest] + [least] * (number_of - 1), total - largest - least * (number_of - 1)
    while spare > 0:
        movable = [i for i in range(1, number_of) if holding[i] < largest] or [i for i in range(1, number_of) if holding[i] < reach]
        whole, budget = sum([weights[i] for i in movable]), spare
        for i in movable:
            more = min(reach - holding[i], max(1, budget * weights[i] // whole), spare)
            holding[i] = holding[i] + more
            spare = spare - more
    return np.array(holding)


def bell_draw(stream_key, dims, deviation, limit, shards=(), held_as=jnp.bfloat16):
    array = jax.random.normal(stream_key, dims, jnp.float32) * deviation
    if len(shards) > 0:
        array = shard_levels(stream_key, dims, shards, -0.22, 0.18) * array
    return jnp.clip(array, min=-limit, max=limit).astype(held_as)


def setup_inputs(seed: int = 0) -> dict:
    key_of = jax.random.split(jax.random.key(seed), 7)
    tokens = bell_draw(key_of[0], (TOKENS, D), 1.0, 6.0, ((0, 16), (1, 2)))
    expert_ids_keys = jax.random.split(jax.random.fold_in(key_of[1], 1), TOKENS // TOK)
    expert_ids_turns = jax.random.permutation(jax.random.fold_in(key_of[1], 3), TOKENS // TOK)
    expert_ids = jax.vmap(lambda own, number: shared_out(jax.random.fold_in(key_of[1], 2), own, number, TOK, EXPERTS, TOPK, CAP, 1))(expert_ids_keys, expert_ids_turns).reshape((TOKENS, TOPK))
    gate_levels = set_ends(jax.random.randint(key_of[2], (TOKENS, TOPK), 1, 4096), jax.random.fold_in(key_of[2], 1), 1, 4095).astype(jnp.int32)
    gate_weight = bell_draw(key_of[3], (N_GRP, D, H // 2), D ** -0.5, 0.0625, ((0, 4), (1, 2), (2, 4)))
    up_weight = bell_draw(key_of[4], (N_GRP, D, H // 2), D ** -0.5, 0.0625, ((0, 4), (1, 2), (2, 4)))
    down_weight = bell_draw(key_of[5], (N_GRP, H // 2, D), H ** -0.5, 0.125, ((0, 4), (1, 4), (2, 2)))
    return dict(tokens=tokens, expert_ids=expert_ids, gate_levels=gate_levels, gate_weight=gate_weight, up_weight=up_weight, down_weight=down_weight)


ROUTED_SCALE = 2.5


def run_expert(packed):
    rows, w_gate, w_up, w_down = packed
    gate = jnp.dot(rows, w_gate, preferred_element_type=jnp.float32)
    up = jnp.dot(rows, w_up, preferred_element_type=jnp.float32)
    hidden = (jax.nn.silu(gate) * up).astype(jnp.bfloat16)
    return jnp.dot(hidden, w_down, preferred_element_type=jnp.float32).astype(jnp.bfloat16)


def reference(tokens, expert_ids, gate_levels, gate_weight, up_weight, down_weight):
    half = H // 2
    full_gate = gate_weight.reshape(EXPERTS, 2, D, half).transpose(0, 2, 1, 3).reshape(EXPERTS, D, H)
    full_up = up_weight.reshape(EXPERTS, 2, D, half).transpose(0, 2, 1, 3).reshape(EXPERTS, D, H)
    full_down = down_weight.reshape(EXPERTS, H, D)
    per_block = TOK * TOPK
    picks = expert_ids.reshape(-1, per_block)
    blocks = picks.shape[0]
    same = picks[:, :, None] == picks[:, None, :]
    order = jnp.arange(per_block, dtype=jnp.int32)
    earlier = order[None, :] < order[:, None]
    rank = jnp.sum(jnp.logical_and(same, earlier[None]), axis=2).astype(jnp.int32)
    block_ids = jnp.arange(blocks, dtype=jnp.int32)
    place = ((block_ids % N_TP) * N_GRP + block_ids // N_TP) * CAP
    rows_each = N_TP * N_GRP * CAP
    slot = (picks * rows_each + place[:, None] + rank).reshape(-1).astype(jnp.int32)
    token_of = jnp.repeat(jnp.arange(TOKENS, dtype=jnp.int32), TOPK)
    table = jnp.zeros((EXPERTS * rows_each, D), jnp.bfloat16).at[slot].set(tokens[token_of])
    table = table.reshape(EXPERTS, rows_each, D)
    outputs = lax.map(run_expert, (table, full_gate, full_up, full_down)).reshape(-1, D)
    picked = outputs[slot].reshape(TOKENS, TOPK, D).astype(jnp.float32)
    levels = gate_levels.astype(jnp.float32)
    weights = ROUTED_SCALE * levels / jnp.sum(levels, axis=1, keepdims=True)
    mixed = jnp.einsum("tk,tkd->td", weights, picked, precision=lax.Precision.HIGHEST)
    return mixed.astype(jnp.bfloat16)
```

```python
import jax
import jax.numpy as jnp
from jax import lax
from jax.sharding import PartitionSpec as P

ROUTED_SCALE = 2.5
LANES = 128
BASE = 64


def pack(tokens, expert_ids, gate_levels):
    high = gate_levels // BASE
    routing = jnp.concatenate([expert_ids, high, gate_levels - high * BASE], axis=1)
    spare = -routing.shape[1] % LANES
    routing = jnp.pad(routing, ((0, 0), (0, spare))).astype(tokens.dtype)
    return jnp.concatenate([tokens, routing], axis=1)


def weight_of(routing, top, expert):
    routing = routing.astype(jnp.float32)
    ids = routing[:, :top]
    levels = routing[:, top : 2 * top] * BASE + routing[:, 2 * top : 3 * top]
    mine = jnp.where(ids == expert.astype(jnp.float32), levels, 0.0)
    return ROUTED_SCALE * jnp.sum(mine, axis=1, keepdims=True) / jnp.sum(levels, axis=1, keepdims=True)


def shift(value, axis, by):
    size = lax.axis_size(axis)
    return lax.ppermute(value, axis, [(i, (i + by) % size) for i in range(size)])


def shift_expert(value, by):
    groups = lax.axis_size("grp")
    return lax.ppermute(value, "grp", [(i, (i + 2 * by) % groups) for i in range(groups)])


def swap_half(value):
    return lax.ppermute(value, "grp", [(i, i ^ 1) for i in range(lax.axis_size("grp"))])


def per_device(tokens, expert_ids, gate_levels, gate_weight, up_weight, down_weight):
    bf16, f32 = jnp.bfloat16, jnp.float32
    experts = lax.axis_size("grp") // 2
    n_tp, n_ex = lax.axis_size("tp"), lax.axis_size("ex")
    count, width = tokens.shape
    top = expert_ids.shape[1]
    expert = lax.axis_index("grp") // 2
    w_both = (gate_weight[0], up_weight[0])
    w_down = down_weight[0]
    inner = w_down.shape[0]

    own = pack(tokens, expert_ids, gate_levels)
    line = jnp.concatenate([own] + [shift(own, "tp", s) for s in range(1, n_tp)], axis=0)
    chunks = [line] + [shift_expert(line, s) for s in range(1, experts)]
    sums = []
    for rows in (chunks[0], jnp.concatenate(chunks[1:], axis=0)):
        rows = jnp.concatenate([rows, swap_half(rows)], axis=0)
        scale = weight_of(rows[:, width:], top, expert)
        rows = rows[:, :width]
        part = jnp.concatenate([jnp.dot(rows, w, preferred_element_type=f32) for w in w_both], axis=1)
        sent = part.astype(bf16)
        for s in range(1, n_ex):
            part = part + shift(sent, "ex", s).astype(f32)
        hidden = (jax.nn.silu(part[:, :inner]) * part[:, inner:]).astype(bf16)
        out = jnp.dot(hidden, w_down, preferred_element_type=f32) * scale
        kept = out.shape[0] // 2
        sums.append(out[:kept] + swap_half(out[kept:].astype(bf16)).astype(f32))
    total = sums[0]
    for s in range(1, experts):
        far = lax.slice_in_dim(sums[1], (s - 1) * n_tp * count, s * n_tp * count, axis=0)
        total = total + shift_expert(far.astype(bf16), -s).astype(f32)
    total = total.reshape(n_tp, count, width)
    mixed = total[0]
    for s in range(1, n_tp):
        mixed = mixed + shift(total[s].astype(bf16), "tp", -s).astype(f32)
    return mixed.astype(bf16)


def solution(mesh):
    return jax.shard_map(
        per_device,
        mesh=mesh,
        in_specs=(
            P(("grp", "tp"), "ex"),
            P(("grp", "tp"), None),
            P(("grp", "tp"), None),
            P("grp", "ex", "tp"),
            P("grp", "ex", "tp"),
            P("grp", "tp", "ex"),
        ),
        out_specs=P(("grp", "tp"), "ex"),
        check_vma=False,
    )
```

```python
import jax
import jax.numpy as jnp
from jax import lax
from jax.experimental import pallas as pl
from jax.sharding import PartitionSpec as P

ROUTED_SCALE = 2.5
LANES = 128
BASE = 64


def pack_kernel(tokens_ref, ids_ref, levels_ref, packed_ref):
    width = tokens_ref.shape[1]
    top = ids_ref.shape[1]
    levels = levels_ref[...]
    high = levels // BASE
    packed_ref[:, :width] = tokens_ref[...]
    lane = lax.broadcasted_iota(jnp.int32, (tokens_ref.shape[0], LANES), 1)
    routing = jnp.zeros(lane.shape, jnp.int32)
    for k, field in enumerate((ids_ref[...], high, levels - high * BASE)):
        for j in range(top):
            routing = jnp.where(lane == k * top + j, field[:, j : j + 1], routing)
    packed_ref[:, width:] = routing.astype(jnp.float32).astype(packed_ref.dtype)


def pack(tokens, expert_ids, gate_levels):
    count, width = tokens.shape
    return pl.pallas_call(
        pack_kernel,
        out_shape=jax.ShapeDtypeStruct((count, width + LANES), tokens.dtype),
    )(tokens, expert_ids, gate_levels)


def weight_of(routing, top, expert):
    routing = routing.astype(jnp.float32)
    ids = routing[:, :top]
    levels = routing[:, top : 2 * top] * BASE + routing[:, 2 * top : 3 * top]
    mine = jnp.where(ids == expert.astype(jnp.float32), levels, 0.0)
    return ROUTED_SCALE * jnp.sum(mine, axis=1, keepdims=True) / jnp.sum(levels, axis=1, keepdims=True)


def shift(value, axis, by):
    size = lax.axis_size(axis)
    return lax.ppermute(value, axis, [(i, (i + by) % size) for i in range(size)])


def shift_expert(value, by):
    groups = lax.axis_size("grp")
    return lax.ppermute(value, "grp", [(i, (i + 2 * by) % groups) for i in range(groups)])


def swap_half(value):
    return lax.ppermute(value, "grp", [(i, i ^ 1) for i in range(lax.axis_size("grp"))])


def per_device(tokens, expert_ids, gate_levels, gate_weight, up_weight, down_weight):
    bf16, f32 = jnp.bfloat16, jnp.float32
    experts = lax.axis_size("grp") // 2
    n_tp, n_ex = lax.axis_size("tp"), lax.axis_size("ex")
    count, width = tokens.shape
    top = expert_ids.shape[1]
    expert = lax.axis_index("grp") // 2
    w_both = (gate_weight[0], up_weight[0])
    w_down = down_weight[0]
    inner = w_down.shape[0]

    def partial_sums(rows):
        part = jnp.concatenate([jnp.dot(rows[:, :width], w, preferred_element_type=f32) for w in w_both], axis=1)
        sent = part.astype(bf16)
        return part, [shift(sent, "ex", s) for s in range(1, n_ex)]

    def partial_out(rows, part, others):
        for other in others:
            part = part + other.astype(f32)
        hidden = (jax.nn.silu(part[:, :inner]) * part[:, inner:]).astype(bf16)
        out = jnp.dot(hidden, w_down, preferred_element_type=f32) * weight_of(rows[:, width:], top, expert)
        kept = out.shape[0] // 2
        return out[:kept] + swap_half(out[kept:].astype(bf16)).astype(f32)

    def sum_over_tp(out):
        out = out.reshape(-1, n_tp, count, width)
        total = out[:, 0]
        for s in range(1, n_tp):
            total = total + shift(out[:, s].astype(bf16), "tp", -s).astype(f32)
        return total

    own = pack(tokens, expert_ids, gate_levels)
    others = jnp.concatenate([shift(own, "tp", s) for s in range(1, n_tp)], axis=0)
    near = jnp.concatenate([own, others], axis=0)
    far = []
    for s in range(1, experts):
        far += [shift_expert(own, s), shift_expert(others, s)]
    far = jnp.concatenate(far, axis=0)
    near = jnp.concatenate([near, swap_half(near)], axis=0)
    far = jnp.concatenate([far, swap_half(far)], axis=0)
    near_parts = partial_sums(near)
    far_parts = partial_sums(far)
    mixed = sum_over_tp(partial_out(near, *near_parts))[0]
    far_out = sum_over_tp(partial_out(far, *far_parts))
    for s in range(1, experts):
        mixed = mixed + shift_expert(far_out[s - 1].astype(bf16), -s).astype(f32)
    return mixed.astype(bf16)


def solution(mesh):
    return jax.shard_map(
        per_device,
        mesh=mesh,
        in_specs=(
            P(("grp", "tp"), "ex"),
            P(("grp", "tp"), None),
            P(("grp", "tp"), None),
            P("grp", "ex", "tp"),
            P("grp", "ex", "tp"),
            P("grp", "tp", "ex"),
        ),
        out_specs=P(("grp", "tp"), "ex"),
        check_vma=False,
    )
```

```python
import jax
import jax.numpy as jnp
from jax import lax
from jax.experimental import pallas as pl
from jax.experimental.pallas import tpu as pltpu
from jax.sharding import PartitionSpec as P

ROUTED_SCALE = 2.5
LANES = 128
BASE = 64


def pack_kernel(tokens_ref, ids_ref, levels_ref, packed_ref):
    count, width = tokens_ref.shape
    top = ids_ref.shape[0]
    packed_ref[:, :width] = tokens_ref[...]
    row = lax.broadcasted_iota(jnp.int32, (count, count), 0)
    column = lax.broadcasted_iota(jnp.int32, (count, count), 1)
    lane = lax.broadcasted_iota(jnp.int32, (count, LANES), 1)
    levels = levels_ref[...]
    high = levels // BASE
    routing = jnp.zeros(lane.shape, jnp.int32)
    for k, field in enumerate((ids_ref[...], high, levels - high * BASE)):
        for j in range(top):
            upright = jnp.sum(jnp.where(row == column, field[j : j + 1, :], 0), axis=1, keepdims=True)
            routing = jnp.where(lane == k * top + j, upright, routing)
    packed_ref[:, width:] = routing.astype(jnp.float32).astype(packed_ref.dtype)


def pack(tokens, expert_ids, gate_levels):
    count, width = tokens.shape
    return pl.pallas_call(
        pack_kernel,
        out_shape=jax.ShapeDtypeStruct((count, width + LANES), tokens.dtype),
        compiler_params=pltpu.CompilerParams(vmem_limit_bytes=2 * 1024 * 1024),
    )(tokens, expert_ids.T, gate_levels.T)


def weight_of(routing, top, expert):
    routing = routing.astype(jnp.float32)
    ids = routing[:, :top]
    levels = routing[:, top : 2 * top] * BASE + routing[:, 2 * top : 3 * top]
    mine = jnp.where(ids == expert.astype(jnp.float32), levels, 0.0)
    return ROUTED_SCALE * jnp.sum(mine, axis=1, keepdims=True) / jnp.sum(levels, axis=1, keepdims=True)


def shift(value, axis, by):
    size = lax.axis_size(axis)
    return lax.ppermute(value, axis, [(i, (i + by) % size) for i in range(size)])


def shift_expert(value, by_expert, by_tp=0):
    groups, n_tp = lax.axis_size("grp"), lax.axis_size("tp")
    pairs = []
    for g in range(groups):
        for t in range(n_tp):
            to = (g + 2 * by_expert) % groups * n_tp + (t + by_tp) % n_tp
            pairs.append((g * n_tp + t, to))
    return lax.ppermute(value, ("grp", "tp"), pairs)


def swap_half(value):
    return lax.ppermute(value, "grp", [(i, i ^ 1) for i in range(lax.axis_size("grp"))])


def after(value, earlier):
    first = earlier[(0,) * earlier.ndim]
    return jnp.where(first != first, jnp.zeros_like(value), value)


def per_device(tokens, expert_ids, gate_levels, gate_weight, up_weight, down_weight):
    bf16, f32 = jnp.bfloat16, jnp.float32
    experts = lax.axis_size("grp") // 2
    n_tp, n_ex = lax.axis_size("tp"), lax.axis_size("ex")
    count, width = tokens.shape
    top = expert_ids.shape[1]
    expert = lax.axis_index("grp") // 2
    w_both = (gate_weight[0], up_weight[0])
    w_down = down_weight[0]
    inner = w_down.shape[0]

    def partial_sums(rows):
        part = jnp.concatenate([jnp.dot(rows[:, :width], w, preferred_element_type=f32) for w in w_both], axis=1)
        sent = part.astype(bf16)
        return part, [shift(sent, "ex", s) for s in range(1, n_ex)]

    def partial_out(rows, part, others, earlier):
        for other in others:
            part = part + after(other, earlier).astype(f32)
        hidden = (jax.nn.silu(part[:, :inner]) * part[:, inner:]).astype(bf16)
        out = jnp.dot(hidden, w_down, preferred_element_type=f32) * weight_of(rows[:, width:], top, expert)
        kept = out.shape[0] // 2
        return out[:kept] + swap_half(out[kept:].astype(bf16)).astype(f32)

    own = pack(tokens, expert_ids, gate_levels)
    line = jnp.concatenate([own] + [shift(own, "tp", s) for s in range(1, n_tp)], axis=0)
    far = [shift_expert(line, s) for s in range(1, experts)]
    near = jnp.concatenate([line, swap_half(line)], axis=0)
    near_parts = partial_sums(near)
    far = after(jnp.concatenate(far, axis=0), near_parts[0])
    far = jnp.concatenate([far, swap_half(far)], axis=0)
    far_parts = partial_sums(far)
    near_out = partial_out(near, *near_parts, far_parts[0]).reshape(n_tp, count, width)
    mixed = near_out[0]
    for t in range(1, n_tp):
        mixed = mixed + shift(near_out[t].astype(bf16), "tp", -t).astype(f32)
    far_out = partial_out(far, *far_parts, near_out).reshape(experts - 1, n_tp, count, width).astype(bf16)
    for s in range(1, experts):
        for t in range(n_tp):
            mixed = mixed + shift_expert(far_out[s - 1, t], -s, -t).astype(f32)
    return mixed.astype(bf16)


def solution(mesh):
    return jax.shard_map(
        per_device,
        mesh=mesh,
        in_specs=(
            P(("grp", "tp"), "ex"),
            P(("grp", "tp"), None),
            P(("grp", "tp"), None),
            P("grp", "ex", "tp"),
            P("grp", "ex", "tp"),
            P("grp", "tp", "ex"),
        ),
        out_specs=P(("grp", "tp"), "ex"),
        check_vma=False,
    )
```

```python
import jax
import jax.numpy as jnp
from jax import lax
from jax.experimental import pallas as pl
from jax.experimental.pallas import tpu as pltpu
from jax.sharding import PartitionSpec as P

ROUTED_SCALE = 2.5
LANES = 128
BASE = 64


def pack_kernel(tokens_hbm, ids_hbm, levels_hbm, packed_ref, ids_ref, levels_ref, sems):
    count, width = tokens_hbm.shape
    top = ids_ref.shape[0]
    copies = [
        pltpu.make_async_copy(tokens_hbm, packed_ref.at[:, pl.ds(0, width)], sems.at[0]),
        pltpu.make_async_copy(ids_hbm, ids_ref, sems.at[1]),
        pltpu.make_async_copy(levels_hbm, levels_ref, sems.at[2]),
    ]
    for copy in copies:
        copy.start()
    row = lax.broadcasted_iota(jnp.int32, (count, count), 0)
    column = lax.broadcasted_iota(jnp.int32, (count, count), 1)
    lane = lax.broadcasted_iota(jnp.int32, (count, LANES), 1)
    routing = jnp.zeros(lane.shape, jnp.int32)
    for copy in copies[1:]:
        copy.wait()
    levels = levels_ref[...]
    high = levels // BASE
    for k, field in enumerate((ids_ref[...], high, levels - high * BASE)):
        for j in range(top):
            upright = jnp.sum(jnp.where(row == column, field[j : j + 1, :], 0), axis=1, keepdims=True)
            routing = jnp.where(lane == k * top + j, upright, routing)
    packed_ref[:, width:] = routing.astype(jnp.float32).astype(packed_ref.dtype)
    copies[0].wait()


def pack(tokens, expert_ids, gate_levels):
    count, width = tokens.shape
    top = expert_ids.shape[1]
    return pl.pallas_call(
        pack_kernel,
        out_shape=jax.ShapeDtypeStruct((count, width + LANES), tokens.dtype),
        in_specs=[pl.BlockSpec(memory_space=pltpu.HBM)] * 3,
        out_specs=pl.BlockSpec(memory_space=pltpu.VMEM),
        scratch_shapes=[
            pltpu.VMEM((top, count), jnp.int32),
            pltpu.VMEM((top, count), jnp.int32),
            pltpu.SemaphoreType.DMA((3,)),
        ],
    )(tokens, expert_ids.T, gate_levels.T)


def weight_of(routing, top, expert):
    routing = routing.astype(jnp.float32)
    ids = routing[:, :top]
    levels = routing[:, top : 2 * top] * BASE + routing[:, 2 * top : 3 * top]
    mine = jnp.where(ids == expert.astype(jnp.float32), levels, 0.0)
    return ROUTED_SCALE * jnp.sum(mine, axis=1, keepdims=True) / jnp.sum(levels, axis=1, keepdims=True)


def shift(value, axis, by):
    size = lax.axis_size(axis)
    return lax.ppermute(value, axis, [(i, (i + by) % size) for i in range(size)])


def shift_expert(value, by_expert, by_tp=0):
    groups, n_tp = lax.axis_size("grp"), lax.axis_size("tp")
    pairs = []
    for g in range(groups):
        for t in range(n_tp):
            to = (g + 2 * by_expert) % groups * n_tp + (t + by_tp) % n_tp
            pairs.append((g * n_tp + t, to))
    return lax.ppermute(value, ("grp", "tp"), pairs)


def swap_half(value):
    return lax.ppermute(value, "grp", [(i, i ^ 1) for i in range(lax.axis_size("grp"))])


def hand_on(*refs):
    del refs


def after(value, *earlier):
    return pl.pallas_call(
        hand_on,
        out_shape=jax.ShapeDtypeStruct(value.shape, value.dtype),
        in_specs=[pl.BlockSpec(memory_space=pl.ANY)] * (1 + len(earlier)),
        out_specs=pl.BlockSpec(memory_space=pl.ANY),
        input_output_aliases={0: 0},
        compiler_params=pltpu.CompilerParams(vmem_limit_bytes=1024 * 1024),
    )(value, *earlier)


def per_device(tokens, expert_ids, gate_levels, gate_weight, up_weight, down_weight):
    bf16, f32 = jnp.bfloat16, jnp.float32
    experts = lax.axis_size("grp") // 2
    n_tp, n_ex = lax.axis_size("tp"), lax.axis_size("ex")
    count, width = tokens.shape
    top = expert_ids.shape[1]
    expert = lax.axis_index("grp") // 2
    w_both = (gate_weight[0], up_weight[0])
    w_down = down_weight[0]
    inner = w_down.shape[0]

    def partial_sums(rows):
        part = jnp.concatenate([jnp.dot(rows[:, :width], w, preferred_element_type=f32) for w in w_both], axis=1)
        sent = part.astype(bf16)
        return part, sent, [shift(sent, "ex", s) for s in range(1, n_ex)]

    def partial_out(rows, part, others):
        for other in others:
            part = part + other.astype(f32)
        hidden = (jax.nn.silu(part[:, :inner]) * part[:, inner:]).astype(bf16)
        out = jnp.dot(hidden, w_down, preferred_element_type=f32) * weight_of(rows[:, width:], top, expert)
        kept = out.shape[0] // 2
        return out[:kept], swap_half(out[kept:].astype(bf16))

    own = pack(tokens, expert_ids, gate_levels)
    far = jnp.concatenate([shift_expert(own, s, t) for s in range(1, experts) for t in range(n_tp)], axis=0)
    near = [shift(own, "tp", t) for t in range(1, n_tp)]
    far = jnp.concatenate([far, swap_half(far)], axis=0)
    far_part, far_sent, far_others = partial_sums(far)
    near = jnp.concatenate([own] + [after(rows, far_sent) for rows in near], axis=0)
    near_swapped = swap_half(near)
    far_others = [after(other, near) for other in far_others]
    far_kept, far_swapped = partial_out(far, far_part, far_others)
    near = jnp.concatenate([near, near_swapped], axis=0)
    near_part, near_sent, near_others = partial_sums(near)
    far_out = far_kept + after(far_swapped, near_sent).astype(f32)
    far_out = far_out.reshape(experts - 1, n_tp, count, width).astype(bf16)
    far_back = [shift_expert(far_out[s - 1, t], -s, -t) for s in range(1, experts) for t in range(n_tp)]
    near_others = [after(other, far_out) for other in near_others]
    near_kept, near_swapped = partial_out(near, near_part, near_others)
    near_out = near_kept + near_swapped.astype(f32)
    near_out = near_out.reshape(n_tp, count, width)
    near_back = [shift(near_out[t].astype(bf16), "tp", -t) for t in range(1, n_tp)]
    mixed = near_out[0]
    for back in far_back + near_back:
        mixed = mixed + back.astype(f32)
    return mixed.astype(bf16)


def solution(mesh):
    return jax.shard_map(
        per_device,
        mesh=mesh,
        in_specs=(
            P(("grp", "tp"), "ex"),
            P(("grp", "tp"), None),
            P(("grp", "tp"), None),
            P("grp", "ex", "tp"),
            P("grp", "ex", "tp"),
            P("grp", "tp", "ex"),
        ),
        out_specs=P(("grp", "tp"), "ex"),
        check_vma=False,
    )
```

```python
import functools

import jax
import jax.numpy as jnp
from jax import lax
from jax.experimental import pallas as pl
from jax.experimental.pallas import tpu as pltpu
from jax.sharding import PartitionSpec as P

ROUTED_SCALE = 2.5
MIB = 1024 * 1024


def shift(value, axis, by):
    size = lax.axis_size(axis)
    return lax.ppermute(value, axis, [(i, (i + by) % size) for i in range(size)])


def shift_expert(value, by_expert, by_tp=0):
    groups, n_tp = lax.axis_size("grp"), lax.axis_size("tp")
    pairs = []
    for g in range(groups):
        for t in range(n_tp):
            to = (g + 2 * by_expert) % groups * n_tp + (t + by_tp) % n_tp
            pairs.append((g * n_tp + t, to))
    return lax.ppermute(value, ("grp", "tp"), pairs)


def swap_half(value):
    return lax.ppermute(value, "grp", [(i, i ^ 1) for i in range(lax.axis_size("grp"))])


def hand_on(*refs):
    del refs


def after(value, *earlier):
    return pl.pallas_call(
        hand_on,
        out_shape=jax.ShapeDtypeStruct(value.shape, value.dtype),
        in_specs=[pl.BlockSpec(memory_space=pl.ANY)] * (1 + len(earlier)),
        out_specs=pl.BlockSpec(memory_space=pl.ANY),
        input_output_aliases={0: 0},
        compiler_params=pltpu.CompilerParams(vmem_limit_bytes=MIB),
    )(value, *earlier)


def copy_kernel(from_ref, to_ref):
    to_ref[...] = from_ref[...]


def copied(value):
    return pl.pallas_call(
        copy_kernel,
        out_shape=jax.ShapeDtypeStruct(value.shape, value.dtype),
        compiler_params=pltpu.CompilerParams(vmem_limit_bytes=2 * MIB),
    )(value)


def mix_kernel(n_tp, experts, ids_ref, levels_ref, *refs):
    *piece_refs, mixed_ref = refs
    count = mixed_ref.shape[0]
    expert = lax.axis_index("grp") // 2
    row = lax.broadcasted_iota(jnp.int32, (count, count), 0)
    column = lax.broadcasted_iota(jnp.int32, (count, count), 1)
    ids = ids_ref[...]
    levels = levels_ref[...].astype(jnp.float32)
    whole = jnp.sum(levels, axis=0, keepdims=True)
    mixed = jnp.zeros(mixed_ref.shape, jnp.float32)
    for s in range(experts):
        source = lax.rem(expert - s + experts, experts)
        weight = ROUTED_SCALE * jnp.sum(jnp.where(ids == source, levels, 0.0), axis=0, keepdims=True) / whole
        upright = jnp.sum(jnp.where(row == column, weight, 0.0), axis=1, keepdims=True)
        total = piece_refs[s * n_tp][...].astype(jnp.float32)
        for t in range(1, n_tp):
            total = total + piece_refs[s * n_tp + t][...].astype(jnp.float32)
        mixed = mixed + upright * total.astype(jnp.bfloat16).astype(jnp.float32)
    mixed_ref[...] = mixed.astype(mixed_ref.dtype)


def mix(expert_ids, gate_levels, pieces, n_tp, experts):
    return pl.pallas_call(
        functools.partial(mix_kernel, n_tp, experts),
        out_shape=jax.ShapeDtypeStruct(pieces[0].shape, jnp.bfloat16),
        compiler_params=pltpu.CompilerParams(vmem_limit_bytes=12 * MIB),
    )(expert_ids.T, gate_levels.T, *pieces)


def per_device(tokens, expert_ids, gate_levels, gate_weight, up_weight, down_weight):
    bf16, f32 = jnp.bfloat16, jnp.float32
    experts = lax.axis_size("grp") // 2
    n_tp, n_ex = lax.axis_size("tp"), lax.axis_size("ex")
    count, width = tokens.shape
    w_gate, w_up, w_down = gate_weight[0], up_weight[0], down_weight[0]
    inner = w_down.shape[0]

    def partial_sums(rows):
        parts = [jnp.dot(rows, w, preferred_element_type=f32) for w in (w_gate, w_up)]
        part = jnp.concatenate(parts, axis=1)
        sent = part.astype(bf16)
        return part, sent, [shift(sent, "ex", s) for s in range(1, n_ex)]

    def partial_out(part, others):
        for other in others:
            part = part + other.astype(f32)
        hidden = (jax.nn.silu(part[:, :inner]) * part[:, inner:]).astype(bf16)
        out = jnp.dot(hidden, w_down, preferred_element_type=f32)
        kept = out.shape[0] // 2
        return out[:kept] + swap_half(out[kept:].astype(bf16)).astype(f32)

    held = copied(tokens)
    blocks = [held] + [shift(tokens, "tp", t) for t in (n_tp - 1, *range(1, n_tp - 1))]
    first, rest = jnp.concatenate(blocks[:2], axis=0), jnp.concatenate(blocks[2:], axis=0)
    far_first = [shift_expert(first, s) for s in range(1, experts)]
    far_rest = [shift_expert(rest, s) for s in range(1, experts)]
    near = jnp.concatenate([first, rest], axis=0)
    near = jnp.concatenate([near, swap_half(near)], axis=0)
    near_part, near_sent, near_others = partial_sums(near)
    far = []
    for one, two in zip(far_first, far_rest):
        far += [one, after(two, near_sent)]
    far = jnp.concatenate(far, axis=0)
    far = jnp.concatenate([far, swap_half(far)], axis=0)
    far_part, far_sent, far_others = partial_sums(far)
    places = (0, n_tp - 1, *range(1, n_tp - 1))
    near_out = partial_out(near_part, [after(other, far_sent) for other in near_others])
    near_out = near_out.reshape(n_tp, count, width)
    near_sent = near_out[1:].astype(bf16)
    pieces = [near_out[0]] + [shift(near_sent[i], "tp", -t) for i, t in enumerate(places[1:])]
    far_out = partial_out(far_part, [after(other, near_sent) for other in far_others])
    far_out = far_out.reshape(experts - 1, n_tp, count, width).astype(bf16)
    for s in range(1, experts):
        pieces += [shift_expert(far_out[experts - 1 - s, i], s, -t) for i, t in enumerate(places)]
    return mix(expert_ids, gate_levels, pieces, n_tp, experts)


def solution(mesh):
    return jax.shard_map(
        per_device,
        mesh=mesh,
        in_specs=(
            P(("grp", "tp"), "ex"),
            P(("grp", "tp"), None),
            P(("grp", "tp"), None),
            P("grp", "ex", "tp"),
            P("grp", "ex", "tp"),
            P("grp", "tp", "ex"),
        ),
        out_specs=P(("grp", "tp"), "ex"),
        check_vma=False,
    )
```

```python
import functools

import jax
import jax.numpy as jnp
from jax import lax
from jax.experimental import pallas as pl
from jax.experimental.pallas import tpu as pltpu
from jax.sharding import PartitionSpec as P

ROUTED_SCALE = 2.5
MIB = 1024 * 1024


def shift(value, axis, by):
    size = lax.axis_size(axis)
    return lax.ppermute(value, axis, [(i, (i + by) % size) for i in range(size)])


def shift_expert(value, by_expert, by_tp=0):
    groups, n_tp = lax.axis_size("grp"), lax.axis_size("tp")
    pairs = []
    for g in range(groups):
        for t in range(n_tp):
            to = (g + 2 * by_expert) % groups * n_tp + (t + by_tp) % n_tp
            pairs.append((g * n_tp + t, to))
    return lax.ppermute(value, ("grp", "tp"), pairs)


def swap_half(value):
    return lax.ppermute(value, "grp", [(i, i ^ 1) for i in range(lax.axis_size("grp"))])


def hand_on(*refs):
    del refs


def after(value, *earlier, flops=0):
    return pl.pallas_call(
        hand_on,
        out_shape=jax.ShapeDtypeStruct(value.shape, value.dtype),
        in_specs=[pl.BlockSpec(memory_space=pl.ANY)] * (1 + len(earlier)),
        out_specs=pl.BlockSpec(memory_space=pl.ANY),
        input_output_aliases={0: 0},
        cost_estimate=pl.CostEstimate(flops=flops, bytes_accessed=0, transcendentals=0),
        compiler_params=pltpu.CompilerParams(vmem_limit_bytes=MIB),
    )(value, *earlier)


def copy_kernel(from_ref, to_ref):
    to_ref[...] = from_ref[...]


def copied(value):
    return pl.pallas_call(
        copy_kernel,
        out_shape=jax.ShapeDtypeStruct(value.shape, value.dtype),
        compiler_params=pltpu.CompilerParams(vmem_limit_bytes=2 * MIB),
    )(value)


def mix_kernel(n_tp, experts, ids_ref, levels_ref, *refs):
    *piece_refs, mixed_ref = refs
    count = mixed_ref.shape[0]
    expert = lax.axis_index("grp") // 2
    row = lax.broadcasted_iota(jnp.int32, (count, count), 0)
    column = lax.broadcasted_iota(jnp.int32, (count, count), 1)
    ids = ids_ref[...]
    levels = levels_ref[...].astype(jnp.float32)
    whole = jnp.sum(levels, axis=0, keepdims=True)
    mixed = jnp.zeros(mixed_ref.shape, jnp.float32)
    for s in range(experts):
        source = lax.rem(expert - s + experts, experts)
        weight = ROUTED_SCALE * jnp.sum(jnp.where(ids == source, levels, 0.0), axis=0, keepdims=True) / whole
        upright = jnp.sum(jnp.where(row == column, weight, 0.0), axis=1, keepdims=True)
        total = piece_refs[s * n_tp][...].astype(jnp.float32)
        for t in range(1, n_tp):
            total = total + piece_refs[s * n_tp + t][...].astype(jnp.float32)
        mixed = mixed + upright * total.astype(jnp.bfloat16).astype(jnp.float32)
    mixed_ref[...] = mixed.astype(mixed_ref.dtype)


def mix(expert_ids, gate_levels, pieces, n_tp, experts):
    return pl.pallas_call(
        functools.partial(mix_kernel, n_tp, experts),
        out_shape=jax.ShapeDtypeStruct(pieces[0].shape, jnp.bfloat16),
        compiler_params=pltpu.CompilerParams(vmem_limit_bytes=12 * MIB),
    )(expert_ids.T, gate_levels.T, *pieces)


def per_device(tokens, expert_ids, gate_levels, gate_weight, up_weight, down_weight):
    bf16, f32 = jnp.bfloat16, jnp.float32
    experts = lax.axis_size("grp") // 2
    n_tp, n_ex = lax.axis_size("tp"), lax.axis_size("ex")
    count, width = tokens.shape
    w_gate, w_up, w_down = gate_weight[0], up_weight[0], down_weight[0]
    inner = w_down.shape[0]

    def partial_sums(rows):
        parts = [jnp.dot(rows, w, preferred_element_type=f32) for w in (w_gate, w_up)]
        part = jnp.concatenate(parts, axis=1)
        sent = part.astype(bf16)
        return part, sent, [shift(sent, "ex", s) for s in range(1, n_ex)]

    def partial_out(part, others, part_flops, kept_flops):
        if part_flops:
            part = after(part, flops=part_flops)
        for other in others:
            part = part + other.astype(f32)
        hidden = (jax.nn.silu(part[:, :inner]) * part[:, inner:]).astype(bf16)
        out = jnp.dot(hidden, w_down, preferred_element_type=f32)
        kept = out.shape[0] // 2
        swapped = swap_half(out[kept:].astype(bf16)).astype(f32)
        if kept_flops:
            out = after(out, flops=kept_flops)
        return out[:kept] + swapped

    held = copied(tokens)
    blocks = [held] + [shift(tokens, "tp", t) for t in (n_tp - 1, *range(1, n_tp - 1))]
    first, rest = jnp.concatenate(blocks[:2], axis=0), jnp.concatenate(blocks[2:], axis=0)
    far_first = [shift_expert(first, s) for s in range(1, experts)]
    far_rest = [shift_expert(rest, s) for s in range(1, experts)]
    near = jnp.concatenate([first, rest], axis=0)
    near = jnp.concatenate([near, swap_half(near)], axis=0)
    near_part, near_sent, near_others = partial_sums(near)
    far = []
    for one, two in zip(far_first, far_rest):
        far += [one, after(two, near_sent)]
    far = jnp.concatenate(far, axis=0)
    far_swapped = swap_half(far)
    far = jnp.concatenate([after(far, flops=3450000000), far_swapped], axis=0)
    far_part, far_sent, far_others = partial_sums(far)
    places = (0, n_tp - 1, *range(1, n_tp - 1))
    near_out = partial_out(near_part, [after(other, far_sent) for other in near_others], 3450000000, 3450000000)
    near_out = near_out.reshape(n_tp, count, width)
    near_sent = near_out[1:].astype(bf16)
    pieces = [near_out[0]] + [shift(near_sent[i], "tp", -t) for i, t in enumerate(places[1:])]
    far_out = partial_out(far_part, [after(other, *pieces[1:3]) for other in far_others], 0, 0)
    far_out = far_out.reshape(experts - 1, n_tp, count, width).astype(bf16)
    for s in range(1, experts):
        pieces += [shift_expert(far_out[experts - 1 - s, i], s, -t) for i, t in enumerate(places)]
    return mix(expert_ids, gate_levels, pieces, n_tp, experts)


def solution(mesh):
    return jax.shard_map(
        per_device,
        mesh=mesh,
        in_specs=(
            P(("grp", "tp"), "ex"),
            P(("grp", "tp"), None),
            P(("grp", "tp"), None),
            P("grp", "ex", "tp"),
            P("grp", "ex", "tp"),
            P("grp", "tp", "ex"),
        ),
        out_specs=P(("grp", "tp"), "ex"),
        check_vma=False,
    )
```

```python
import functools

import jax
import jax.numpy as jnp
from jax import lax
from jax.experimental import pallas as pl
from jax.experimental.pallas import tpu as pltpu
from jax.sharding import PartitionSpec as P

ROUTED_SCALE = 2.5
LANES = 128
MIB = 1024 * 1024


def shift(value, axis, by):
    size = lax.axis_size(axis)
    return lax.ppermute(value, axis, [(i, (i + by) % size) for i in range(size)])


def shift_expert(value, by):
    groups = lax.axis_size("grp")
    return lax.ppermute(value, "grp", [(i, (i + 2 * by) % groups) for i in range(groups)])


def swap_half(value):
    return lax.ppermute(value, "grp", [(i, i ^ 1) for i in range(lax.axis_size("grp"))])


def joined(parts):
    return parts[0] if len(parts) == 1 else jnp.concatenate(parts, axis=0)


def hand_on(*refs):
    del refs


def after(value, *earlier, flops=0):
    return pl.pallas_call(
        hand_on,
        out_shape=jax.ShapeDtypeStruct(value.shape, value.dtype),
        in_specs=[pl.BlockSpec(memory_space=pl.ANY)] * (1 + len(earlier)),
        out_specs=pl.BlockSpec(memory_space=pl.ANY),
        input_output_aliases={0: 0},
        cost_estimate=pl.CostEstimate(flops=flops, bytes_accessed=0, transcendentals=0),
        compiler_params=pltpu.CompilerParams(vmem_limit_bytes=MIB),
    )(value, *earlier)


def copy_kernel(from_ref, to_ref):
    to_ref[...] = from_ref[...]


def copied(value):
    return pl.pallas_call(
        copy_kernel,
        out_shape=jax.ShapeDtypeStruct(value.shape, value.dtype),
        compiler_params=pltpu.CompilerParams(vmem_limit_bytes=2 * MIB),
    )(value)


def weight_kernel(ids_ref, levels_ref, weight_ref):
    count = weight_ref.shape[0]
    top = ids_ref.shape[0]
    row = lax.broadcasted_iota(jnp.int32, (count, count), 0)
    column = lax.broadcasted_iota(jnp.int32, (count, count), 1)
    lane = lax.broadcasted_iota(jnp.int32, weight_ref.shape, 1)
    levels = levels_ref[...].astype(jnp.float32)
    shares = ROUTED_SCALE * levels / jnp.sum(levels, axis=0, keepdims=True)
    ids = ids_ref[...]
    weight = jnp.zeros(weight_ref.shape, jnp.float32)
    for j in range(top):
        chosen = jnp.sum(jnp.where(row == column, ids[j : j + 1, :], 0), axis=1, keepdims=True)
        share = jnp.sum(jnp.where(row == column, shares[j : j + 1, :], 0.0), axis=1, keepdims=True)
        weight = weight + jnp.where(lane == chosen, share, 0.0)
    weight_ref[...] = weight


def weights_of(expert_ids, gate_levels, experts):
    return pl.pallas_call(
        weight_kernel,
        out_shape=jax.ShapeDtypeStruct((expert_ids.shape[0], -(-experts // LANES) * LANES), jnp.float32),
        compiler_params=pltpu.CompilerParams(vmem_limit_bytes=MIB),
    )(expert_ids.T, gate_levels.T)


def blend_kernel(experts, start, blocks, near_ref, *refs):
    weight_refs, far_refs, out_refs = refs[:blocks], refs[blocks : blocks + experts - 1], refs[blocks + experts - 1 :]
    expert = lax.axis_index("grp") // 2
    count = out_refs[0].shape[0]
    for i in range(blocks):
        weight = weight_refs[i][...]
        lane = lax.broadcasted_iota(jnp.int32, weight.shape, 1)
        mixed = jnp.zeros(out_refs[i].shape, jnp.float32)
        for s in range(experts):
            source = lax.rem(expert + s, experts)
            column = jnp.sum(jnp.where(lane == source, weight, 0.0), axis=1, keepdims=True)
            if s:
                rows = far_refs[s - 1][i * count : (i + 1) * count, :].astype(jnp.float32)
            else:
                rows = near_ref[start + i * count : start + (i + 1) * count, :]
            mixed = mixed + column * rows
        out_refs[i][...] = mixed.astype(out_refs[i].dtype)


def blended(near, start, weights, fars, types):
    count, width = weights[0].shape[0], near.shape[1]
    return pl.pallas_call(
        functools.partial(blend_kernel, len(fars) + 1, start, len(weights)),
        out_shape=[jax.ShapeDtypeStruct((count, width), kind) for kind in types],
        compiler_params=pltpu.CompilerParams(vmem_limit_bytes=16 * MIB),
    )(near, *weights, *fars)


def per_device(tokens, expert_ids, gate_levels, gate_weight, up_weight, down_weight):
    bf16, f32 = jnp.bfloat16, jnp.float32
    experts = lax.axis_size("grp") // 2
    n_tp, n_ex = lax.axis_size("tp"), lax.axis_size("ex")
    count, width = tokens.shape
    w_gate, w_up, w_down = gate_weight[0], up_weight[0], down_weight[0]
    inner = w_down.shape[0]
    others = range(1, experts)

    def partial_sums(rows):
        part = jnp.concatenate([jnp.dot(rows, w, preferred_element_type=f32) for w in (w_gate, w_up)], axis=1)
        sent = part.astype(bf16)
        return part, sent, [shift(sent, "ex", s) for s in range(1, n_ex)]

    def partial_out(part, others, part_flops, kept_flops):
        if part_flops:
            part = after(part, flops=part_flops)
        for other in others:
            part = part + other.astype(f32)
        hidden = (jax.nn.silu(part[:, :inner]) * part[:, inner:]).astype(bf16)
        out = jnp.dot(hidden, w_down, preferred_element_type=f32)
        kept = out.shape[0] // 2
        swapped = swap_half(out[kept:].astype(bf16)).astype(f32)
        if kept_flops:
            out = after(out, flops=kept_flops)
        return out[:kept] + swapped

    held = copied(tokens)
    places = tuple(range(1, n_tp))
    rest = joined([shift(tokens, "tp", t) for t in places])
    far_own = [shift_expert(held, s) for s in others]
    far_rest = [shift_expert(rest, s) for s in others]
    near = joined([held, rest])
    near_swapped = swap_half(near)
    near = joined([near, near_swapped])
    near_part, near_sent, near_others = partial_sums(near)
    far = joined([rows for own, other in zip(far_own, far_rest) for rows in (own, after(other, near_sent))])
    far_swapped = swap_half(far)
    far = joined([after(far, flops=3450000000), far_swapped])
    far_part, far_sent, far_others = partial_sums(far)
    near_out = partial_out(near_part, [after(other, far_sent) for other in near_others], 3450000000, 3450000000)
    far_out = partial_out(far_part, [after(other, near_out) for other in far_others], 0, 0).astype(bf16)
    own_weight = weights_of(expert_ids, gate_levels, experts)
    weights = [shift(own_weight, "tp", t) for t in places]
    line, half = n_tp * count, 2 * count
    back_b = [shift_expert(far_out[(s - 1) * line + half : s * line], -s) for s in others]
    back_a = [shift_expert(far_out[(s - 1) * line : (s - 1) * line + half], -s) for s in others]
    pieces_b = blended(near_out, half, weights[1:], back_b, [bf16] * (n_tp - 2))
    own, piece_a = blended(near_out, 0, [own_weight, weights[0]], back_a, [f32, bf16])
    mixed = own
    for t, piece in zip(places, [piece_a, *pieces_b]):
        mixed = mixed + shift(piece, "tp", -t).astype(f32)
    return mixed.astype(bf16)


def solution(mesh):
    return jax.shard_map(
        per_device,
        mesh=mesh,
        in_specs=(
            P(("grp", "tp"), "ex"),
            P(("grp", "tp"), None),
            P(("grp", "tp"), None),
            P("grp", "ex", "tp"),
            P("grp", "ex", "tp"),
            P("grp", "tp", "ex"),
        ),
        out_specs=P(("grp", "tp"), "ex"),
        check_vma=False,
    )
```

```python
import functools

import jax
import jax.numpy as jnp
from jax import lax
from jax.experimental import pallas as pl
from jax.experimental.pallas import tpu as pltpu
from jax.sharding import PartitionSpec as P

ROUTED_SCALE = 2.5
LANES = 128
MIB = 1024 * 1024


def shift(value, axis, by):
    size = lax.axis_size(axis)
    return lax.ppermute(value, axis, [(i, (i + by) % size) for i in range(size)])


def shift_expert(value, by):
    groups = lax.axis_size("grp")
    return lax.ppermute(value, "grp", [(i, (i + 2 * by) % groups) for i in range(groups)])


def swap_half(value):
    return lax.ppermute(value, "grp", [(i, i ^ 1) for i in range(lax.axis_size("grp"))])


def joined(parts):
    return parts[0] if len(parts) == 1 else jnp.concatenate(parts, axis=0)


def hand_on(*refs):
    del refs


def after(value, *earlier, flops=0):
    return pl.pallas_call(
        hand_on,
        out_shape=jax.ShapeDtypeStruct(value.shape, value.dtype),
        in_specs=[pl.BlockSpec(memory_space=pl.ANY)] * (1 + len(earlier)),
        out_specs=pl.BlockSpec(memory_space=pl.ANY),
        input_output_aliases={0: 0},
        cost_estimate=pl.CostEstimate(flops=flops, bytes_accessed=0, transcendentals=0),
        compiler_params=pltpu.CompilerParams(vmem_limit_bytes=MIB),
    )(value, *earlier)


def copy_kernel(from_ref, to_ref):
    to_ref[...] = from_ref[...]


def copied(value):
    return pl.pallas_call(
        copy_kernel,
        out_shape=jax.ShapeDtypeStruct(value.shape, value.dtype),
        compiler_params=pltpu.CompilerParams(vmem_limit_bytes=2 * MIB),
    )(value)


def weight_kernel(ids_ref, levels_ref, weight_ref):
    count = weight_ref.shape[0]
    top = ids_ref.shape[0]
    row = lax.broadcasted_iota(jnp.int32, (count, count), 0)
    column = lax.broadcasted_iota(jnp.int32, (count, count), 1)
    lane = lax.broadcasted_iota(jnp.int32, weight_ref.shape, 1)
    levels = levels_ref[...].astype(jnp.float32)
    shares = ROUTED_SCALE * levels / jnp.sum(levels, axis=0, keepdims=True)
    ids = ids_ref[...]
    weight = jnp.zeros(weight_ref.shape, jnp.float32)
    for j in range(top):
        chosen = jnp.sum(jnp.where(row == column, ids[j : j + 1, :], 0), axis=1, keepdims=True)
        share = jnp.sum(jnp.where(row == column, shares[j : j + 1, :], 0.0), axis=1, keepdims=True)
        weight = weight + jnp.where(lane == chosen, share, 0.0)
    weight_ref[...] = weight


def weights_of(expert_ids, gate_levels, experts):
    return pl.pallas_call(
        weight_kernel,
        out_shape=jax.ShapeDtypeStruct((expert_ids.shape[0], -(-experts // LANES) * LANES), jnp.float32),
        compiler_params=pltpu.CompilerParams(vmem_limit_bytes=MIB),
    )(expert_ids.T, gate_levels.T)


def blend_kernel(experts, start, blocks, near_ref, *refs):
    weight_refs, far_refs, out_refs = refs[:blocks], refs[blocks : blocks + experts - 1], refs[blocks + experts - 1 :]
    expert = lax.axis_index("grp") // 2
    count = out_refs[0].shape[0]
    for i in range(blocks):
        weight = weight_refs[i][...]
        lane = lax.broadcasted_iota(jnp.int32, weight.shape, 1)
        mixed = jnp.zeros(out_refs[i].shape, jnp.float32)
        for s in range(experts):
            source = lax.rem(expert + s, experts)
            column = jnp.sum(jnp.where(lane == source, weight, 0.0), axis=1, keepdims=True)
            if s:
                rows = far_refs[s - 1][i * count : (i + 1) * count, :].astype(jnp.float32)
            else:
                rows = near_ref[start + i * count : start + (i + 1) * count, :]
            mixed = mixed + column * rows
        out_refs[i][...] = mixed.astype(out_refs[i].dtype)


def blended(near, start, weights, fars, types):
    count, width = weights[0].shape[0], near.shape[1]
    return pl.pallas_call(
        functools.partial(blend_kernel, len(fars) + 1, start, len(weights)),
        out_shape=[jax.ShapeDtypeStruct((count, width), kind) for kind in types],
        compiler_params=pltpu.CompilerParams(vmem_limit_bytes=16 * MIB),
    )(near, *weights, *fars)


def per_device(tokens, expert_ids, gate_levels, gate_weight, up_weight, down_weight):
    bf16, f32 = jnp.bfloat16, jnp.float32
    experts = lax.axis_size("grp") // 2
    n_tp, n_ex = lax.axis_size("tp"), lax.axis_size("ex")
    count, width = tokens.shape
    w_gate, w_up, w_down = gate_weight[0], up_weight[0], down_weight[0]
    inner = w_down.shape[0]
    others = range(1, experts)

    def partial_sums(rows):
        part = jnp.concatenate([jnp.dot(rows, w, preferred_element_type=f32) for w in (w_gate, w_up)], axis=1)
        sent = part.astype(bf16)
        return part, sent, [shift(sent, "ex", s) for s in range(1, n_ex)]

    def partial_out(part, others, kept_flops, *earlier):
        for other in others:
            part = part + other.astype(f32)
        hidden = (jax.nn.silu(part[:, :inner]) * part[:, inner:]).astype(bf16)
        out = jnp.dot(hidden, w_down, preferred_element_type=f32)
        kept = out.shape[0] // 2
        swapped = swap_half(out[kept:].astype(bf16)).astype(f32)
        kept_out = after(out, *earlier, flops=kept_flops)[:kept]
        return out, kept_out + swapped

    held = copied(tokens)
    places = tuple(range(1, n_tp))
    blocks = [held] + [shift(tokens, "tp", t) for t in places]
    own_weight = weights_of(expert_ids, gate_levels, experts)
    far = [[shift_expert(rows, s) for rows in blocks] for s in others]
    near = joined(blocks)
    near_swapped = swap_half(after(near, *(line[1] for line in far)))
    near = joined([near, near_swapped])
    near_part, near_sent, near_others = partial_sums(near)
    far = joined([after(rows, near_sent) if i == n_tp - 1 else rows for line in far for i, rows in enumerate(line)])
    far_swapped = swap_half(far)
    far = joined([after(far, flops=3450000000), far_swapped])
    far_part, far_sent, far_others = partial_sums(far)
    near_whole, near_out = partial_out(near_part, [after(other, far_sent) for other in near_others], 3450000000)
    weights = [own_weight] + [shift(after(own_weight, near_whole if i < 1 else near_out), "tp", t) for i, t in enumerate(places)]
    _, far_out = partial_out(far_part, [after(other, near_out, *weights[9:]) for other in far_others], 3450000000, *weights[1:])
    far_out = far_out.astype(bf16)
    far_out = far_out.reshape(experts - 1, n_tp, count, width)
    pieces = []
    for i in reversed(range(n_tp)):
        back = [shift_expert(far_out[s - 1, i], -s) for s in others]
        pieces += blended(near_out, i * count, [weights[i]], back, [bf16 if i else f32])
    own = pieces[-1]
    mixed = own
    for t, piece in zip(reversed(places), pieces):
        mixed = mixed + shift(piece, "tp", -t).astype(f32)
    return mixed.astype(bf16)


def solution(mesh):
    return jax.shard_map(
        per_device,
        mesh=mesh,
        in_specs=(
            P(("grp", "tp"), "ex"),
            P(("grp", "tp"), None),
            P(("grp", "tp"), None),
            P("grp", "ex", "tp"),
            P("grp", "ex", "tp"),
            P("grp", "tp", "ex"),
        ),
        out_specs=P(("grp", "tp"), "ex"),
        check_vma=False,
    )
```

```python
import functools

import jax
import jax.numpy as jnp
from jax import lax
from jax.experimental import pallas as pl
from jax.experimental.pallas import tpu as pltpu
from jax.sharding import PartitionSpec as P

ROUTED_SCALE = 2.5
MIB = 1024 * 1024


def shift(value, axis, by):
    size = lax.axis_size(axis)
    return lax.ppermute(value, axis, [(i, (i + by) % size) for i in range(size)])


def shift_expert(value, by_expert, by_tp=0):
    groups, n_tp = lax.axis_size("grp"), lax.axis_size("tp")
    pairs = []
    for g in range(groups):
        for t in range(n_tp):
            to = (g + 2 * by_expert) % groups * n_tp + (t + by_tp) % n_tp
            pairs.append((g * n_tp + t, to))
    return lax.ppermute(value, ("grp", "tp"), pairs)


def swap_half(value):
    return lax.ppermute(value, "grp", [(i, i ^ 1) for i in range(lax.axis_size("grp"))])


def hand_on(*refs):
    del refs


def after(value, *earlier, flops=0):
    return pl.pallas_call(
        hand_on,
        out_shape=jax.ShapeDtypeStruct(value.shape, value.dtype),
        in_specs=[pl.BlockSpec(memory_space=pl.ANY)] * (1 + len(earlier)),
        out_specs=pl.BlockSpec(memory_space=pl.ANY),
        input_output_aliases={0: 0},
        cost_estimate=pl.CostEstimate(flops=flops, bytes_accessed=0, transcendentals=0),
        compiler_params=pltpu.CompilerParams(vmem_limit_bytes=MIB),
    )(value, *earlier)


def copy_kernel(from_ref, to_ref):
    to_ref[...] = from_ref[...]


def copied(value):
    return pl.pallas_call(
        copy_kernel,
        out_shape=jax.ShapeDtypeStruct(value.shape, value.dtype),
        compiler_params=pltpu.CompilerParams(vmem_limit_bytes=2 * MIB),
    )(value)


def mix_kernel(n_tp, experts, ids_ref, levels_ref, *refs):
    *piece_refs, mixed_ref = refs
    count = mixed_ref.shape[0]
    expert = lax.axis_index("grp") // 2
    row = lax.broadcasted_iota(jnp.int32, (count, count), 0)
    column = lax.broadcasted_iota(jnp.int32, (count, count), 1)
    ids = ids_ref[...]
    levels = levels_ref[...].astype(jnp.float32)
    whole = jnp.sum(levels, axis=0, keepdims=True)
    mixed = jnp.zeros(mixed_ref.shape, jnp.float32)
    for s in range(experts):
        source = lax.rem(expert - s + experts, experts)
        weight = ROUTED_SCALE * jnp.sum(jnp.where(ids == source, levels, 0.0), axis=0, keepdims=True) / whole
        upright = jnp.sum(jnp.where(row == column, weight, 0.0), axis=1, keepdims=True)
        total = piece_refs[s * n_tp][...].astype(jnp.float32)
        for t in range(1, n_tp):
            total = total + piece_refs[s * n_tp + t][...].astype(jnp.float32)
        mixed = mixed + upright * total.astype(jnp.bfloat16).astype(jnp.float32)
    mixed_ref[...] = mixed.astype(mixed_ref.dtype)


def mix(expert_ids, gate_levels, pieces, n_tp, experts):
    return pl.pallas_call(
        functools.partial(mix_kernel, n_tp, experts),
        out_shape=jax.ShapeDtypeStruct(pieces[0].shape, jnp.bfloat16),
        compiler_params=pltpu.CompilerParams(vmem_limit_bytes=12 * MIB),
    )(expert_ids.T, gate_levels.T, *pieces)


def per_device(tokens, expert_ids, gate_levels, gate_weight, up_weight, down_weight):
    bf16, f32 = jnp.bfloat16, jnp.float32
    experts = lax.axis_size("grp") // 2
    n_tp, n_ex = lax.axis_size("tp"), lax.axis_size("ex")
    count, width = tokens.shape
    w_gate, w_up, w_down = gate_weight[0], up_weight[0], down_weight[0]
    inner = w_down.shape[0]

    def partial_sums(rows):
        parts = [jnp.dot(rows, w, preferred_element_type=f32) for w in (w_gate, w_up)]
        part = jnp.concatenate(parts, axis=1)
        sent = part.astype(bf16)
        return part, sent, [shift(sent, "ex", s) for s in range(1, n_ex)]

    def partial_out(part, others, kept_flops):
        for other in others:
            part = part + other.astype(f32)
        hidden = (jax.nn.silu(part[:, :inner]) * part[:, inner:]).astype(bf16)
        out = jnp.dot(hidden, w_down, preferred_element_type=f32)
        kept = out.shape[0] // 2
        swapped = swap_half(out[kept:].astype(bf16)).astype(f32)
        if kept_flops:
            out = after(out, flops=kept_flops)
        return out[:kept] + swapped

    held = copied(tokens)
    places = tuple(range(n_tp))
    blocks = [held] + [shift(tokens, "tp", t) for t in places[1:]]
    far = [[shift_expert(rows, s) for rows in blocks] for s in range(1, experts)]
    near = jnp.concatenate(blocks, axis=0)
    near_swapped = swap_half(after(near, *(line[1] for line in far)))
    near = jnp.concatenate([near, near_swapped], axis=0)
    near_part, near_sent, near_others = partial_sums(near)
    far = [after(rows, near_sent) if i == n_tp - 1 else rows for line in far for i, rows in enumerate(line)]
    far = jnp.concatenate(far, axis=0)
    far_swapped = swap_half(far)
    far = jnp.concatenate([after(far, flops=3450000000), far_swapped], axis=0)
    far_part, far_sent, far_others = partial_sums(far)
    near_out = partial_out(near_part, [after(other, far_sent) for other in near_others], 3450000000)
    near_out = near_out.reshape(n_tp, count, width)
    near_sent = near_out[1:].astype(bf16)
    pieces = [near_out[0]] + [shift(near_sent[i], "tp", -t) for i, t in enumerate(places[1:])]
    far_out = partial_out(far_part, [after(other, near_sent) for other in far_others], 0)
    far_out = far_out.reshape(experts - 1, n_tp, count, width).astype(bf16)
    for s in range(1, experts):
        pieces += [shift_expert(far_out[experts - 1 - s, i], s, -t) for i, t in enumerate(places)]
    return mix(expert_ids, gate_levels, pieces, n_tp, experts)


def solution(mesh):
    return jax.shard_map(
        per_device,
        mesh=mesh,
        in_specs=(
            P(("grp", "tp"), "ex"),
            P(("grp", "tp"), None),
            P(("grp", "tp"), None),
            P("grp", "ex", "tp"),
            P("grp", "ex", "tp"),
            P("grp", "tp", "ex"),
        ),
        out_specs=P(("grp", "tp"), "ex"),
        check_vma=False,
    )
```

```python
import functools

import jax
import jax.numpy as jnp
from jax import lax
from jax.experimental import pallas as pl
from jax.experimental.pallas import tpu as pltpu
from jax.sharding import PartitionSpec as P

ROUTED_SCALE = 2.5
MIB = 1024 * 1024


def shift(value, axis, by):
    size = lax.axis_size(axis)
    return lax.ppermute(value, axis, [(i, (i + by) % size) for i in range(size)])


def shift_expert(value, by_expert, by_tp=0):
    groups, n_tp = lax.axis_size("grp"), lax.axis_size("tp")
    pairs = []
    for g in range(groups):
        for t in range(n_tp):
            to = (g + 2 * by_expert) % groups * n_tp + (t + by_tp) % n_tp
            pairs.append((g * n_tp + t, to))
    return lax.ppermute(value, ("grp", "tp"), pairs)


def swap_half(value):
    return lax.ppermute(value, "grp", [(i, i ^ 1) for i in range(lax.axis_size("grp"))])


def joined(parts):
    return parts[0] if len(parts) == 1 else jnp.concatenate(parts, axis=0)


def hand_on(*refs):
    del refs


def after(value, *earlier, flops=0):
    return pl.pallas_call(
        hand_on,
        out_shape=jax.ShapeDtypeStruct(value.shape, value.dtype),
        in_specs=[pl.BlockSpec(memory_space=pl.ANY)] * (1 + len(earlier)),
        out_specs=pl.BlockSpec(memory_space=pl.ANY),
        input_output_aliases={0: 0},
        cost_estimate=pl.CostEstimate(flops=flops, bytes_accessed=0, transcendentals=0),
        compiler_params=pltpu.CompilerParams(vmem_limit_bytes=MIB),
    )(value, *earlier)


def copy_kernel(from_ref, to_ref):
    to_ref[...] = from_ref[...]


def copied(value):
    return pl.pallas_call(
        copy_kernel,
        out_shape=jax.ShapeDtypeStruct(value.shape, value.dtype),
        compiler_params=pltpu.CompilerParams(vmem_limit_bytes=2 * MIB),
    )(value)


def mix_kernel(n_tp, experts, ids_ref, levels_ref, *refs):
    *piece_refs, mixed_ref = refs
    count = mixed_ref.shape[0]
    expert = lax.axis_index("grp") // 2
    row = lax.broadcasted_iota(jnp.int32, (count, count), 0)
    column = lax.broadcasted_iota(jnp.int32, (count, count), 1)
    ids = ids_ref[...]
    levels = levels_ref[...].astype(jnp.float32)
    whole = jnp.sum(levels, axis=0, keepdims=True)
    mixed = jnp.zeros(mixed_ref.shape, jnp.float32)
    for s in range(experts):
        source = lax.rem(expert - s + experts, experts)
        weight = ROUTED_SCALE * jnp.sum(jnp.where(ids == source, levels, 0.0), axis=0, keepdims=True) / whole
        upright = jnp.sum(jnp.where(row == column, weight, 0.0), axis=1, keepdims=True)
        total = piece_refs[s * n_tp][...].astype(jnp.float32)
        for t in range(1, n_tp):
            total = total + piece_refs[s * n_tp + t][...].astype(jnp.float32)
        mixed = mixed + upright * total.astype(jnp.bfloat16).astype(jnp.float32)
    mixed_ref[...] = mixed.astype(mixed_ref.dtype)


def mix(expert_ids, gate_levels, pieces, n_tp, experts):
    return pl.pallas_call(
        functools.partial(mix_kernel, n_tp, experts),
        out_shape=jax.ShapeDtypeStruct(pieces[0].shape, jnp.bfloat16),
        compiler_params=pltpu.CompilerParams(vmem_limit_bytes=12 * MIB),
    )(expert_ids.T, gate_levels.T, *pieces)


def per_device(tokens, expert_ids, gate_levels, gate_weight, up_weight, down_weight):
    bf16, f32 = jnp.bfloat16, jnp.float32
    experts = lax.axis_size("grp") // 2
    n_tp, n_ex = lax.axis_size("tp"), lax.axis_size("ex")
    count, width = tokens.shape
    w_gate, w_up, w_down = gate_weight[0], up_weight[0], down_weight[0]
    inner = w_down.shape[0]

    def partial_sums(rows):
        parts = [jnp.dot(rows, w, preferred_element_type=f32) for w in (w_gate, w_up)]
        part = jnp.concatenate(parts, axis=1)
        sent = part.astype(bf16)
        return part, sent, [shift(sent, "ex", s) for s in range(1, n_ex)]

    def partial_out(part, others, part_flops, kept_flops):
        if part_flops:
            part = after(part, flops=part_flops)
        for other in others:
            part = part + other.astype(f32)
        hidden = (jax.nn.silu(part[:, :inner]) * part[:, inner:]).astype(bf16)
        out = jnp.dot(hidden, w_down, preferred_element_type=f32)
        kept = out.shape[0] // 2
        swapped = swap_half(out[kept:].astype(bf16)).astype(f32)
        kept_out = after(out, flops=kept_flops) if kept_flops else out
        return out, kept_out[:kept] + swapped

    held = copied(tokens)
    places = (0, 1, *range(n_tp - 1, 1, -1))
    blocks = [held] + [shift(tokens, "tp", t) for t in places[1:]]
    far = [[shift_expert(rows, s) for rows in blocks] for s in range(1, experts)]
    first = joined(blocks[:-1])
    first_swapped = swap_half(after(first, *(line[0] for line in far)))
    first = joined([first, first_swapped])
    a_part, a_sent, a_others = partial_sums(first)
    second = [blocks[-1]] + [after(rows, a_sent) for line in far for i, rows in enumerate(line)]
    second = joined(second)
    second_swapped = swap_half(second)
    a_whole, a_out = partial_out(a_part, [other for other in a_others], 3450000000, 3450000000)
    second = joined([after(second, a_whole, flops=3450000000), second_swapped])
    b_part, b_sent, b_others = partial_sums(second)
    a_out = a_out.reshape(n_tp - 1, count, width)
    a_back = a_out[1:].astype(bf16)
    near = [a_out[0]] + [shift(a_back[i], "tp", -t) for i, t in enumerate(places[1:-1])]
    _, b_out = partial_out(b_part, [after(other, a_back) for other in b_others], 0, 3450000000)
    b_out = b_out.astype(bf16).reshape(-1, count, width)
    near.append(shift(b_out[0], "tp", -places[-1]))
    pieces = near
    for s in range(1, experts):
        pieces = pieces + [shift_expert(b_out[1 + (experts - 1 - s) * n_tp + i], s, -t) for i, t in enumerate(places)]
    return mix(expert_ids, gate_levels, pieces, n_tp, experts)


def solution(mesh):
    return jax.shard_map(
        per_device,
        mesh=mesh,
        in_specs=(
            P(("grp", "tp"), "ex"),
            P(("grp", "tp"), None),
            P(("grp", "tp"), None),
            P("grp", "ex", "tp"),
            P("grp", "ex", "tp"),
            P("grp", "tp", "ex"),
        ),
        out_specs=P(("grp", "tp"), "ex"),
        check_vma=False,
    )
```

```python
import functools

import jax
import jax.numpy as jnp
from jax import lax
from jax.experimental import pallas as pl
from jax.experimental.pallas import tpu as pltpu
from jax.sharding import PartitionSpec as P

ROUTED_SCALE = 2.5
MIB = 1024 * 1024


def shift(value, axis, by):
    size = lax.axis_size(axis)
    return lax.ppermute(value, axis, [(i, (i + by) % size) for i in range(size)])


def shift_expert(value, by_expert, by_tp=0):
    groups, n_tp = lax.axis_size("grp"), lax.axis_size("tp")
    pairs = []
    for g in range(groups):
        for t in range(n_tp):
            to = (g + 2 * by_expert) % groups * n_tp + (t + by_tp) % n_tp
            pairs.append((g * n_tp + t, to))
    return lax.ppermute(value, ("grp", "tp"), pairs)


def swap_half(value):
    return lax.ppermute(value, "grp", [(i, i ^ 1) for i in range(lax.axis_size("grp"))])


def hand_on(*refs):
    del refs


def after(value, *earlier, flops=0):
    return pl.pallas_call(
        hand_on,
        out_shape=jax.ShapeDtypeStruct(value.shape, value.dtype),
        in_specs=[pl.BlockSpec(memory_space=pl.ANY)] * (1 + len(earlier)),
        out_specs=pl.BlockSpec(memory_space=pl.ANY),
        input_output_aliases={0: 0},
        cost_estimate=pl.CostEstimate(flops=flops, bytes_accessed=0, transcendentals=0),
        compiler_params=pltpu.CompilerParams(vmem_limit_bytes=MIB),
    )(value, *earlier)


def copy_kernel(from_ref, to_ref):
    to_ref[...] = from_ref[...]


def copied(value):
    return pl.pallas_call(
        copy_kernel,
        out_shape=jax.ShapeDtypeStruct(value.shape, value.dtype),
        compiler_params=pltpu.CompilerParams(vmem_limit_bytes=2 * MIB),
    )(value)


def mix_kernel(n_tp, experts, ids_ref, levels_ref, *refs):
    *piece_refs, mixed_ref = refs
    piece_refs = piece_refs[::-1]
    count = mixed_ref.shape[0]
    expert = lax.axis_index("grp") // 2
    row = lax.broadcasted_iota(jnp.int32, (count, count), 0)
    column = lax.broadcasted_iota(jnp.int32, (count, count), 1)
    ids = ids_ref[...]
    levels = levels_ref[...].astype(jnp.float32)
    whole = jnp.sum(levels, axis=0, keepdims=True)
    mixed = jnp.zeros(mixed_ref.shape, jnp.float32)
    for s in range(experts):
        source = lax.rem(expert - s + experts, experts)
        weight = ROUTED_SCALE * jnp.sum(jnp.where(ids == source, levels, 0.0), axis=0, keepdims=True) / whole
        upright = jnp.sum(jnp.where(row == column, weight, 0.0), axis=1, keepdims=True)
        total = piece_refs[s * n_tp][...].astype(jnp.float32)
        for t in range(1, n_tp):
            total = total + piece_refs[s * n_tp + t][...].astype(jnp.float32)
        mixed = mixed + upright * total.astype(jnp.bfloat16).astype(jnp.float32)
    mixed_ref[...] = mixed.astype(mixed_ref.dtype)


def mix(expert_ids, gate_levels, pieces, n_tp, experts):
    return pl.pallas_call(
        functools.partial(mix_kernel, n_tp, experts),
        out_shape=jax.ShapeDtypeStruct(pieces[0].shape, jnp.bfloat16),
        compiler_params=pltpu.CompilerParams(vmem_limit_bytes=12 * MIB),
    )(expert_ids.T, gate_levels.T, *pieces)


def per_device(tokens, expert_ids, gate_levels, gate_weight, up_weight, down_weight):
    bf16, f32 = jnp.bfloat16, jnp.float32
    experts = lax.axis_size("grp") // 2
    n_tp, n_ex = lax.axis_size("tp"), lax.axis_size("ex")
    count, width = tokens.shape
    w_gate, w_up, w_down = gate_weight[0], up_weight[0], down_weight[0]
    inner = w_down.shape[0]

    def partial_sums(rows):
        parts = [jnp.dot(rows, w, preferred_element_type=f32) for w in (w_gate, w_up)]
        part = jnp.concatenate(parts, axis=1)
        sent = part.astype(bf16)
        return part, sent, [shift(sent, "ex", s) for s in range(1, n_ex)]

    def partial_out(part, others, kept_flops, part_flops=0, *earlier):
        if part_flops:
            part = after(part, flops=part_flops)
        for other in others:
            part = part + other.astype(f32)
        hidden = (jax.nn.silu(part[:, :inner]) * part[:, inner:]).astype(bf16)
        out = jnp.dot(hidden, w_down, preferred_element_type=f32)
        kept = out.shape[0] // 2
        swapped = swap_half(out[kept:].astype(bf16)).astype(f32)
        kept_out = after(out, flops=kept_flops) if kept_flops else out
        return kept_out, kept_out[:kept] + swapped

    held = copied(tokens)
    places = tuple(range(n_tp))
    blocks = [held] + [shift(tokens, "tp", t) for t in places[1:]]
    far = [[shift_expert(rows, s) for rows in blocks] for s in range(1, experts)]
    near = jnp.concatenate(blocks, axis=0)
    near_swapped = swap_half(after(near, *(line[1] for line in far)))
    near = jnp.concatenate([near, near_swapped], axis=0)
    near_part, near_sent, near_others = partial_sums(near)
    far = [after(rows, near_sent) if i == n_tp - 1 else rows for line in far for i, rows in enumerate(line)]
    far = jnp.concatenate(far, axis=0)
    far_swapped = swap_half(far)
    far = jnp.concatenate([after(far, flops=3450000000), far_swapped], axis=0)
    far_part, far_sent, far_others = partial_sums(far)
    _, near_out = partial_out(near_part, [after(other, far_sent) for other in near_others], 3450000000, 3450000000)
    near_out = near_out.reshape(n_tp, count, width)
    near_sent = near_out[1:].astype(bf16)
    far_whole, far_out = partial_out(far_part, [after(other, near_sent) for other in far_others], 3450000000, 3450000000)
    near_sent = [after(near_sent[i], far_whole) if i in (1, 2) else near_sent[i] for i in range(n_tp - 1)]
    pieces = [near_out[0]] + [shift(near_sent[i], "tp", -t) for i, t in enumerate(places[1:])]
    far_out = far_out.reshape(experts - 1, n_tp, count, width).astype(bf16)
    for s in range(1, experts):
        pieces += [shift_expert(far_out[experts - 1 - s, i], s, -t) for i, t in enumerate(places)]
    return mix(expert_ids, gate_levels, pieces[::-1], n_tp, experts)


def solution(mesh):
    return jax.shard_map(
        per_device,
        mesh=mesh,
        in_specs=(
            P(("grp", "tp"), "ex"),
            P(("grp", "tp"), None),
            P(("grp", "tp"), None),
            P("grp", "ex", "tp"),
            P("grp", "ex", "tp"),
            P("grp", "tp", "ex"),
        ),
        out_specs=P(("grp", "tp"), "ex"),
        check_vma=False,
    )
```

```python
import jax
import jax.numpy as jnp
from jax import lax
from jax.experimental import pallas as pl
from jax.experimental.pallas import tpu as pltpu
from jax.sharding import PartitionSpec as P

ROUTED_SCALE = 2.5
LANES = 128
BASE = 64
MIB = 1024 * 1024


def pack_kernel(tokens_hbm, ids_hbm, levels_hbm, packed_hbm, ids_ref, levels_ref, routing_ref, sems):
    count, width = tokens_hbm.shape
    top = ids_ref.shape[0]
    body = pltpu.make_async_copy(tokens_hbm, packed_hbm.at[:, pl.ds(0, width)], sems.at[0])
    fields = [
        pltpu.make_async_copy(ids_hbm, ids_ref, sems.at[1]),
        pltpu.make_async_copy(levels_hbm, levels_ref, sems.at[2]),
    ]
    for copy in (*fields, body):
        copy.start()
    row = lax.broadcasted_iota(jnp.int32, (count, count), 0)
    column = lax.broadcasted_iota(jnp.int32, (count, count), 1)
    lane = lax.broadcasted_iota(jnp.int32, (count, LANES), 1)
    routing = jnp.zeros(lane.shape, jnp.int32)
    for copy in fields:
        copy.wait()
    levels = levels_ref[...]
    high = levels // BASE
    for k, field in enumerate((ids_ref[...], high, levels - high * BASE)):
        for j in range(top):
            upright = jnp.sum(jnp.where(row == column, field[j : j + 1, :], 0), axis=1, keepdims=True)
            routing = jnp.where(lane == k * top + j, upright, routing)
    routing_ref[...] = routing.astype(jnp.float32).astype(routing_ref.dtype)
    tail = pltpu.make_async_copy(routing_ref, packed_hbm.at[:, pl.ds(width, LANES)], sems.at[3])
    tail.start()
    tail.wait()
    body.wait()


def pack(tokens, expert_ids, gate_levels):
    count, width = tokens.shape
    top = expert_ids.shape[1]
    return pl.pallas_call(
        pack_kernel,
        out_shape=jax.ShapeDtypeStruct((count, width + LANES), tokens.dtype),
        in_specs=[pl.BlockSpec(memory_space=pl.ANY)] * 3,
        out_specs=pl.BlockSpec(memory_space=pl.ANY),
        scratch_shapes=[
            pltpu.VMEM((top, count), jnp.int32),
            pltpu.VMEM((top, count), jnp.int32),
            pltpu.VMEM((count, LANES), tokens.dtype),
            pltpu.SemaphoreType.DMA((4,)),
        ],
    )(tokens, expert_ids.T, gate_levels.T)


def weight_of(routing, top, expert):
    routing = routing.astype(jnp.float32)
    ids = routing[:, :top]
    levels = routing[:, top : 2 * top] * BASE + routing[:, 2 * top : 3 * top]
    mine = jnp.where(ids == expert.astype(jnp.float32), levels, 0.0)
    return ROUTED_SCALE * jnp.sum(mine, axis=1, keepdims=True) / jnp.sum(levels, axis=1, keepdims=True)


def shift(value, axis, by):
    size = lax.axis_size(axis)
    return lax.ppermute(value, axis, [(i, (i + by) % size) for i in range(size)])


def shift_expert(value, by):
    groups = lax.axis_size("grp")
    return lax.ppermute(value, "grp", [(i, (i + 2 * by) % groups) for i in range(groups)])


def swap_half(value):
    return lax.ppermute(value, "grp", [(i, i ^ 1) for i in range(lax.axis_size("grp"))])


def joined(parts):
    return parts[0] if len(parts) == 1 else jnp.concatenate(parts, axis=0)


def hand_on(*refs):
    del refs


def after(value, *earlier, flops=0):
    return pl.pallas_call(
        hand_on,
        out_shape=jax.ShapeDtypeStruct(value.shape, value.dtype),
        in_specs=[pl.BlockSpec(memory_space=pl.ANY)] * (1 + len(earlier)),
        out_specs=pl.BlockSpec(memory_space=pl.ANY),
        input_output_aliases={0: 0},
        cost_estimate=pl.CostEstimate(flops=flops, bytes_accessed=0, transcendentals=0),
        compiler_params=pltpu.CompilerParams(vmem_limit_bytes=MIB),
    )(value, *earlier)


def copy_kernel(from_ref, to_ref):
    to_ref[...] = from_ref[...]


def copied(value):
    return pl.pallas_call(
        copy_kernel,
        out_shape=jax.ShapeDtypeStruct(value.shape, value.dtype),
        compiler_params=pltpu.CompilerParams(vmem_limit_bytes=2 * MIB),
    )(value)


def per_device(tokens, expert_ids, gate_levels, gate_weight, up_weight, down_weight):
    bf16, f32 = jnp.bfloat16, jnp.float32
    experts = lax.axis_size("grp") // 2
    n_tp, n_ex = lax.axis_size("tp"), lax.axis_size("ex")
    count, width = tokens.shape
    top = expert_ids.shape[1]
    expert = lax.axis_index("grp") // 2
    w_gate, w_up, w_down = gate_weight[0], up_weight[0], down_weight[0]
    inner = w_down.shape[0]
    others = range(1, experts)

    def partial_sums(rows):
        part = jnp.concatenate([jnp.dot(rows[:, :width], w, preferred_element_type=f32) for w in (w_gate, w_up)], axis=1)
        sent = part.astype(bf16)
        return part, sent, [shift(sent, "ex", s) for s in range(1, n_ex)]

    def partial_out(rows, part, others, part_flops, kept_flops):
        if part_flops:
            part = after(part, flops=part_flops)
        for other in others:
            part = part + other.astype(f32)
        hidden = (jax.nn.silu(part[:, :inner]) * part[:, inner:]).astype(bf16)
        out = jnp.dot(hidden, w_down, preferred_element_type=f32) * weight_of(rows[:, width:], top, expert)
        kept = out.shape[0] // 2
        swapped = swap_half(out[kept:].astype(bf16)).astype(f32)
        if kept_flops:
            out = after(out, flops=kept_flops)
        return out[:kept] + swapped

    packed = pack(tokens, expert_ids, gate_levels)
    held = copied(packed)
    places = (0, n_tp - 1, *range(1, n_tp - 1))
    blocks = [held] + [shift(packed, "tp", t) for t in places[1:]]
    far = [[shift_expert(rows, s) for rows in blocks] for s in others]
    near = joined(blocks)
    near_swapped = swap_half(after(near, *(line[1] for line in far)))
    near = joined([near, near_swapped])
    near_part, near_sent, near_others = partial_sums(near)
    far = joined([after(rows, near_sent) if i == n_tp - 1 else rows for line in far for i, rows in enumerate(line)])
    far_swapped = swap_half(far)
    far = joined([after(far, flops=3450000000), far_swapped])
    far_part, far_sent, far_others = partial_sums(far)
    near_out = partial_out(near, near_part, [after(other, far_sent) for other in near_others], 3450000000, 3450000000)
    far_out = partial_out(far, far_part, [after(other, near_out) for other in far_others], 0, 0)
    near_out = near_out.reshape(n_tp, count, width)
    far_out = far_out.astype(bf16).reshape(experts - 1, n_tp * count, width)
    line = near_out
    for s in others:
        line = line + shift_expert(far_out[s - 1], -s).astype(f32).reshape(n_tp, count, width)
    mixed = line[0]
    for i in range(1, n_tp):
        mixed = mixed + shift(line[i].astype(bf16), "tp", -places[i]).astype(f32)
    return mixed.astype(bf16)


def solution(mesh):
    return jax.shard_map(
        per_device,
        mesh=mesh,
        in_specs=(
            P(("grp", "tp"), "ex"),
            P(("grp", "tp"), None),
            P(("grp", "tp"), None),
            P("grp", "ex", "tp"),
            P("grp", "ex", "tp"),
            P("grp", "tp", "ex"),
        ),
        out_specs=P(("grp", "tp"), "ex"),
        check_vma=False,
    )
```

```python
import functools

import jax
import jax.numpy as jnp
from jax import lax
from jax.experimental import pallas as pl
from jax.experimental.pallas import tpu as pltpu
from jax.sharding import PartitionSpec as P

ROUTED_SCALE = 2.5
MIB = 1024 * 1024


def shift(value, axis, by):
    size = lax.axis_size(axis)
    return lax.ppermute(value, axis, [(i, (i + by) % size) for i in range(size)])


def shift_expert(value, by_expert, by_tp=0):
    groups, n_tp = lax.axis_size("grp"), lax.axis_size("tp")
    pairs = []
    for g in range(groups):
        for t in range(n_tp):
            to = (g + 2 * by_expert) % groups * n_tp + (t + by_tp) % n_tp
            pairs.append((g * n_tp + t, to))
    return lax.ppermute(value, ("grp", "tp"), pairs)


def swap_half(value):
    return lax.ppermute(value, "grp", [(i, i ^ 1) for i in range(lax.axis_size("grp"))])


def hand_on(*refs):
    del refs


def after(value, *earlier, flops=0):
    return pl.pallas_call(
        hand_on,
        out_shape=jax.ShapeDtypeStruct(value.shape, value.dtype),
        in_specs=[pl.BlockSpec(memory_space=pl.ANY)] * (1 + len(earlier)),
        out_specs=pl.BlockSpec(memory_space=pl.ANY),
        input_output_aliases={0: 0},
        cost_estimate=pl.CostEstimate(flops=flops, bytes_accessed=0, transcendentals=0),
        compiler_params=pltpu.CompilerParams(vmem_limit_bytes=MIB),
    )(value, *earlier)


def copy_kernel(from_ref, to_ref):
    to_ref[...] = from_ref[...]


def copied(value):
    return pl.pallas_call(
        copy_kernel,
        out_shape=jax.ShapeDtypeStruct(value.shape, value.dtype),
        compiler_params=pltpu.CompilerParams(vmem_limit_bytes=2 * MIB),
    )(value)


def mix_kernel(n_tp, experts, ids_ref, levels_ref, *refs):
    *piece_refs, mixed_ref = refs
    piece_refs = piece_refs[: n_tp] + [r for s in range(1, experts) for r in piece_refs[s * n_tp : (s + 1) * n_tp][::-1]]
    count = mixed_ref.shape[0]
    expert = lax.axis_index("grp") // 2
    row = lax.broadcasted_iota(jnp.int32, (count, count), 0)
    column = lax.broadcasted_iota(jnp.int32, (count, count), 1)
    ids = ids_ref[...]
    levels = levels_ref[...].astype(jnp.float32)
    whole = jnp.sum(levels, axis=0, keepdims=True)
    mixed = jnp.zeros(mixed_ref.shape, jnp.float32)
    for s in range(experts):
        source = lax.rem(expert - s + experts, experts)
        weight = ROUTED_SCALE * jnp.sum(jnp.where(ids == source, levels, 0.0), axis=0, keepdims=True) / whole
        upright = jnp.sum(jnp.where(row == column, weight, 0.0), axis=1, keepdims=True)
        total = piece_refs[s * n_tp][...].astype(jnp.float32)
        for t in range(1, n_tp):
            total = total + piece_refs[s * n_tp + t][...].astype(jnp.float32)
        mixed = mixed + upright * total.astype(jnp.bfloat16).astype(jnp.float32)
    mixed_ref[...] = mixed.astype(mixed_ref.dtype)


def mix(expert_ids, gate_levels, pieces, n_tp, experts):
    return pl.pallas_call(
        functools.partial(mix_kernel, n_tp, experts),
        out_shape=jax.ShapeDtypeStruct(pieces[0].shape, jnp.bfloat16),
        compiler_params=pltpu.CompilerParams(vmem_limit_bytes=12 * MIB),
    )(expert_ids.T, gate_levels.T, *pieces)


def per_device(tokens, expert_ids, gate_levels, gate_weight, up_weight, down_weight):
    bf16, f32 = jnp.bfloat16, jnp.float32
    experts = lax.axis_size("grp") // 2
    n_tp, n_ex = lax.axis_size("tp"), lax.axis_size("ex")
    count, width = tokens.shape
    w_gate, w_up, w_down = gate_weight[0], up_weight[0], down_weight[0]
    inner = w_down.shape[0]

    def partial_sums(rows):
        parts = [jnp.dot(rows, w, preferred_element_type=f32) for w in (w_gate, w_up)]
        part = jnp.concatenate(parts, axis=1)
        sent = part.astype(bf16)
        return part, sent, [shift(sent, "ex", s) for s in range(1, n_ex)]

    def partial_out(part, others, kept_flops, part_flops=0, *earlier):
        if part_flops:
            part = after(part, flops=part_flops)
        for other in others:
            part = part + other.astype(f32)
        hidden = (jax.nn.silu(part[:, :inner]) * part[:, inner:]).astype(bf16)
        out = jnp.dot(hidden, w_down, preferred_element_type=f32)
        kept = out.shape[0] // 2
        swapped = swap_half(out[kept:].astype(bf16)).astype(f32)
        kept_out = after(out, flops=kept_flops) if kept_flops else out
        return kept_out, kept_out[:kept] + swapped

    held = copied(tokens)
    places = tuple(range(n_tp))
    blocks = [held] + [shift(tokens, "tp", t) for t in places[1:]]
    far = [[shift_expert(rows, s) for rows in blocks] for s in range(1, experts)]
    near = jnp.concatenate(blocks, axis=0)
    near_swapped = swap_half(after(near, *(line[1] for line in far)))
    near = jnp.concatenate([near, near_swapped], axis=0)
    near_part, near_sent, near_others = partial_sums(near)
    far = [after(rows, near_sent) if i == n_tp - 1 else rows for line in far for i, rows in enumerate(line)]
    far = jnp.concatenate(far, axis=0)
    far_swapped = swap_half(far)
    far = jnp.concatenate([after(far, flops=3450000000), far_swapped], axis=0)
    far_part, far_sent, far_others = partial_sums(far)
    _, near_out = partial_out(near_part, [after(other, far_sent) for other in near_others], 3450000000, 3450000000)
    near_out = near_out.reshape(n_tp, count, width)
    near_sent = near_out[1:].astype(bf16)
    far_whole, far_out = partial_out(far_part, [after(other, near_sent) for other in far_others], 0, 0)
    far_out = far_out.reshape(experts - 1, n_tp, count, width).astype(bf16)
    far_back = []
    for s in range(1, experts):
        far_back += [shift_expert(far_out[experts - 1 - s, i], s, -t) for i, t in enumerate(places)]
    near_sent = after(near_sent, *far_back[::n_tp])
    near_back = [near_out[0]] + [shift(near_sent[i], "tp", -t) for i, t in enumerate(places[1:])]
    pieces = near_back + [piece for s in range(experts - 1) for piece in far_back[s * n_tp : (s + 1) * n_tp][::-1]]
    return mix(expert_ids, gate_levels, pieces, n_tp, experts)


def solution(mesh):
    return jax.shard_map(
        per_device,
        mesh=mesh,
        in_specs=(
            P(("grp", "tp"), "ex"),
            P(("grp", "tp"), None),
            P(("grp", "tp"), None),
            P("grp", "ex", "tp"),
            P("grp", "ex", "tp"),
            P("grp", "tp", "ex"),
        ),
        out_specs=P(("grp", "tp"), "ex"),
        check_vma=False,
    )
```

```python
import functools

import jax
import jax.numpy as jnp
from jax import lax
from jax.experimental import pallas as pl
from jax.experimental.pallas import tpu as pltpu
from jax.sharding import PartitionSpec as P

ROUTED_SCALE = 2.5
MIB = 1024 * 1024


def shift(value, axis, by):
    size = lax.axis_size(axis)
    return lax.ppermute(value, axis, [(i, (i + by) % size) for i in range(size)])


def shift_expert(value, by_expert, by_tp=0):
    groups, n_tp = lax.axis_size("grp"), lax.axis_size("tp")
    pairs = []
    for g in range(groups):
        for t in range(n_tp):
            to = (g + 2 * by_expert) % groups * n_tp + (t + by_tp) % n_tp
            pairs.append((g * n_tp + t, to))
    return lax.ppermute(value, ("grp", "tp"), pairs)


def swap_half(value):
    return lax.ppermute(value, "grp", [(i, i ^ 1) for i in range(lax.axis_size("grp"))])


def hand_on(*refs):
    del refs


def after(value, *earlier, flops=0):
    return pl.pallas_call(
        hand_on,
        out_shape=jax.ShapeDtypeStruct(value.shape, value.dtype),
        in_specs=[pl.BlockSpec(memory_space=pl.ANY)] * (1 + len(earlier)),
        out_specs=pl.BlockSpec(memory_space=pl.ANY),
        input_output_aliases={0: 0},
        cost_estimate=pl.CostEstimate(flops=flops, bytes_accessed=0, transcendentals=0),
        compiler_params=pltpu.CompilerParams(vmem_limit_bytes=MIB),
    )(value, *earlier)


def copy_kernel(from_ref, to_ref):
    to_ref[...] = from_ref[...]


def copied(value):
    return pl.pallas_call(
        copy_kernel,
        out_shape=jax.ShapeDtypeStruct(value.shape, value.dtype),
        compiler_params=pltpu.CompilerParams(vmem_limit_bytes=2 * MIB),
    )(value)


def mix_kernel(n_tp, experts, ids_ref, levels_ref, *refs):
    *piece_refs, mixed_ref = refs
    count = mixed_ref.shape[0]
    expert = lax.axis_index("grp") // 2
    row = lax.broadcasted_iota(jnp.int32, (count, count), 0)
    column = lax.broadcasted_iota(jnp.int32, (count, count), 1)
    ids = ids_ref[...]
    levels = levels_ref[...].astype(jnp.float32)
    whole = jnp.sum(levels, axis=0, keepdims=True)
    mixed = jnp.zeros(mixed_ref.shape, jnp.float32)
    for s in range(experts):
        source = lax.rem(expert - s + experts, experts)
        weight = ROUTED_SCALE * jnp.sum(jnp.where(ids == source, levels, 0.0), axis=0, keepdims=True) / whole
        upright = jnp.sum(jnp.where(row == column, weight, 0.0), axis=1, keepdims=True)
        total = piece_refs[s * n_tp][...].astype(jnp.float32)
        for t in range(1, n_tp):
            total = total + piece_refs[s * n_tp + t][...].astype(jnp.float32)
        mixed = mixed + upright * total.astype(jnp.bfloat16).astype(jnp.float32)
    mixed_ref[...] = mixed.astype(mixed_ref.dtype)


def mix(expert_ids, gate_levels, pieces, n_tp, experts):
    return pl.pallas_call(
        functools.partial(mix_kernel, n_tp, experts),
        out_shape=jax.ShapeDtypeStruct(pieces[0].shape, jnp.bfloat16),
        compiler_params=pltpu.CompilerParams(vmem_limit_bytes=12 * MIB),
    )(expert_ids.T, gate_levels.T, *pieces)


def per_device(tokens, expert_ids, gate_levels, gate_weight, up_weight, down_weight):
    bf16, f32 = jnp.bfloat16, jnp.float32
    experts = lax.axis_size("grp") // 2
    n_tp, n_ex = lax.axis_size("tp"), lax.axis_size("ex")
    count, width = tokens.shape
    w_gate, w_up, w_down = gate_weight[0], up_weight[0], down_weight[0]
    inner = w_down.shape[0]

    def partial_sums(rows):
        parts = [jnp.dot(rows, w, preferred_element_type=f32) for w in (w_gate, w_up)]
        part = jnp.concatenate(parts, axis=1)
        sent = part.astype(bf16)
        return part, sent, [shift(sent, "ex", s) for s in range(1, n_ex)]

    def partial_out(part, others, kept_flops, part_flops=0, *earlier):
        if part_flops:
            part = after(part, flops=part_flops)
        for other in others:
            part = part + other.astype(f32)
        hidden = (jax.nn.silu(part[:, :inner]) * part[:, inner:]).astype(bf16)
        out = jnp.dot(hidden, w_down, preferred_element_type=f32)
        kept = out.shape[0] // 2
        swapped = swap_half(out[kept:].astype(bf16)).astype(f32)
        if kept_flops:
            out = after(after(out, *earlier) if earlier else out, flops=kept_flops)
        return out[:kept] + swapped

    held = copied(tokens)
    places = tuple(range(n_tp))
    blocks = [held] + [shift(tokens, "tp", t) for t in places[1:]]
    far = [[shift_expert(rows, s) for rows in blocks] for s in range(1, experts)]
    near = jnp.concatenate(blocks, axis=0)
    near_swapped = swap_half(after(near, *(line[1] for line in far)))
    near = jnp.concatenate([near, near_swapped], axis=0)
    near_part, near_sent, near_others = partial_sums(near)
    early = jnp.concatenate([rows for line in far for rows in line[:-1]], axis=0)
    early_swapped = swap_half(after(early, near_swapped))
    late = jnp.concatenate([after(line[-1], near_sent) for line in far], axis=0)
    late_swapped = swap_half(late)
    far = jnp.concatenate([early, after(late, flops=3450000000), early_swapped, late_swapped], axis=0)
    far_part, far_sent, far_others = partial_sums(far)
    near_out = partial_out(near_part, [after(other, far_sent) for other in near_others], 3450000000, 3450000000)
    near_out = near_out.reshape(n_tp, count, width)
    near_sent = near_out[1:].astype(bf16)
    pieces = [near_out[0]] + [shift(near_sent[i], "tp", -t) for i, t in enumerate(places[1:])]
    far_out = partial_out(far_part, [after(other, near_sent) for other in far_others], 0, 0)
    far_out = far_out.astype(bf16)
    split = early.shape[0]
    for s in range(1, experts):
        line = experts - 1 - s
        for i, t in enumerate(places):
            start = (line * (n_tp - 1) + i) * count if i < n_tp - 1 else split + line * count
            pieces.append(shift_expert(far_out[start : start + count], s, -t))
    return mix(expert_ids, gate_levels, pieces, n_tp, experts)


def solution(mesh):
    return jax.shard_map(
        per_device,
        mesh=mesh,
        in_specs=(
            P(("grp", "tp"), "ex"),
            P(("grp", "tp"), None),
            P(("grp", "tp"), None),
            P("grp", "ex", "tp"),
            P("grp", "ex", "tp"),
            P("grp", "tp", "ex"),
        ),
        out_specs=P(("grp", "tp"), "ex"),
        check_vma=False,
    )
```

```python
import functools

import jax
import jax.numpy as jnp
from jax import lax
from jax.experimental import pallas as pl
from jax.experimental.pallas import tpu as pltpu
from jax.sharding import PartitionSpec as P

ROUTED_SCALE = 2.5
MIB = 1024 * 1024


def shift(value, axis, by):
    size = lax.axis_size(axis)
    return lax.ppermute(value, axis, [(i, (i + by) % size) for i in range(size)])


def shift_expert(value, by_expert, by_tp=0):
    groups, n_tp = lax.axis_size("grp"), lax.axis_size("tp")
    pairs = []
    for g in range(groups):
        for t in range(n_tp):
            to = (g + 2 * by_expert) % groups * n_tp + (t + by_tp) % n_tp
            pairs.append((g * n_tp + t, to))
    return lax.ppermute(value, ("grp", "tp"), pairs)


def swap_half(value):
    return lax.ppermute(value, "grp", [(i, i ^ 1) for i in range(lax.axis_size("grp"))])


def hand_on(*refs):
    del refs


def after(value, *earlier, flops=0):
    return pl.pallas_call(
        hand_on,
        out_shape=jax.ShapeDtypeStruct(value.shape, value.dtype),
        in_specs=[pl.BlockSpec(memory_space=pl.ANY)] * (1 + len(earlier)),
        out_specs=pl.BlockSpec(memory_space=pl.ANY),
        input_output_aliases={0: 0},
        cost_estimate=pl.CostEstimate(flops=flops, bytes_accessed=0, transcendentals=0),
        compiler_params=pltpu.CompilerParams(vmem_limit_bytes=MIB),
    )(value, *earlier)


def copy_kernel(from_ref, to_ref):
    to_ref[...] = from_ref[...]


def copied(value):
    return pl.pallas_call(
        copy_kernel,
        out_shape=jax.ShapeDtypeStruct(value.shape, value.dtype),
        compiler_params=pltpu.CompilerParams(vmem_limit_bytes=2 * MIB),
    )(value)


def mix_kernel(n_tp, experts, ids_ref, levels_ref, *refs):
    *piece_refs, mixed_ref = refs
    count = mixed_ref.shape[0]
    expert = lax.axis_index("grp") // 2
    row = lax.broadcasted_iota(jnp.int32, (count, count), 0)
    column = lax.broadcasted_iota(jnp.int32, (count, count), 1)
    ids = ids_ref[...]
    levels = levels_ref[...].astype(jnp.float32)
    whole = jnp.sum(levels, axis=0, keepdims=True)
    mixed = jnp.zeros(mixed_ref.shape, jnp.float32)
    for s in range(experts):
        source = lax.rem(expert - s + experts, experts)
        weight = ROUTED_SCALE * jnp.sum(jnp.where(ids == source, levels, 0.0), axis=0, keepdims=True) / whole
        upright = jnp.sum(jnp.where(row == column, weight, 0.0), axis=1, keepdims=True)
        total = piece_refs[s * n_tp][...].astype(jnp.float32)
        for t in range(1, n_tp):
            total = total + piece_refs[s * n_tp + t][...].astype(jnp.float32)
        mixed = mixed + upright * total.astype(jnp.bfloat16).astype(jnp.float32)
    mixed_ref[...] = mixed.astype(mixed_ref.dtype)


def mix(expert_ids, gate_levels, pieces, n_tp, experts):
    return pl.pallas_call(
        functools.partial(mix_kernel, n_tp, experts),
        out_shape=jax.ShapeDtypeStruct(pieces[0].shape, jnp.bfloat16),
        compiler_params=pltpu.CompilerParams(vmem_limit_bytes=12 * MIB),
    )(expert_ids.T, gate_levels.T, *pieces)


def per_device(tokens, expert_ids, gate_levels, gate_weight, up_weight, down_weight):
    bf16, f32 = jnp.bfloat16, jnp.float32
    experts = lax.axis_size("grp") // 2
    n_tp, n_ex = lax.axis_size("tp"), lax.axis_size("ex")
    count, width = tokens.shape
    w_gate, w_up, w_down = gate_weight[0], up_weight[0], down_weight[0]
    inner = w_down.shape[0]

    def partial_sums(rows):
        parts = [jnp.dot(rows, w, preferred_element_type=f32) for w in (w_gate, w_up)]
        part = jnp.concatenate(parts, axis=1)
        sent = part.astype(bf16)
        return part, sent, [shift(sent, "ex", s) for s in range(1, n_ex)]

    def partial_out(part, others, kept_flops, part_flops=0, *earlier):
        if part_flops:
            part = after(part, flops=part_flops)
        for other in others:
            part = part + other.astype(f32)
        hidden = (jax.nn.silu(part[:, :inner]) * part[:, inner:]).astype(bf16)
        out = jnp.dot(hidden, w_down, preferred_element_type=f32)
        kept = out.shape[0] // 2
        swapped = swap_half(out[kept:].astype(bf16)).astype(f32)
        if kept_flops:
            out = after(after(out, *earlier) if earlier else out, flops=kept_flops)
        return out[:kept] + swapped

    held = copied(tokens)
    places = tuple(range(n_tp))
    blocks = [held] + [shift(tokens, "tp", t) for t in places[1:]]
    far = [[shift_expert(rows, s) for rows in blocks] for s in range(1, experts)]
    near = jnp.concatenate(blocks, axis=0)
    near_swapped = swap_half(after(near, *(line[1] for line in far)))
    near = jnp.concatenate([near, near_swapped], axis=0)
    near_part, near_sent, near_others = partial_sums(near)
    last = n_tp - 2
    early = jnp.concatenate([rows for line in far for i, rows in enumerate(line) if i != last], axis=0)
    early_swapped = swap_half(after(early, near_swapped))
    late = jnp.concatenate([after(line[last], near_sent) for line in far], axis=0)
    late_swapped = swap_half(late)
    far = jnp.concatenate([early, after(late, flops=3450000000), early_swapped, late_swapped], axis=0)
    far_part, far_sent, far_others = partial_sums(far)
    near_out = partial_out(near_part, [after(other, far_sent) for other in near_others], 3450000000, 3450000000)
    near_out = near_out.reshape(n_tp, count, width)
    near_sent = near_out[1:].astype(bf16)
    pieces = [near_out[0]] + [shift(near_sent[i], "tp", -t) for i, t in enumerate(places[1:])]
    far_out = partial_out(far_part, [after(other, near_sent) for other in far_others], 0, 0)
    far_out = far_out.astype(bf16)
    split = early.shape[0]
    for s in range(1, experts):
        line = experts - 1 - s
        for i, t in enumerate(places):
            start = split + line * count if i == last else (line * (n_tp - 1) + i - (i > last)) * count
            pieces.append(shift_expert(far_out[start : start + count], s, -t))
    return mix(expert_ids, gate_levels, pieces, n_tp, experts)


def solution(mesh):
    return jax.shard_map(
        per_device,
        mesh=mesh,
        in_specs=(
            P(("grp", "tp"), "ex"),
            P(("grp", "tp"), None),
            P(("grp", "tp"), None),
            P("grp", "ex", "tp"),
            P("grp", "ex", "tp"),
            P("grp", "tp", "ex"),
        ),
        out_specs=P(("grp", "tp"), "ex"),
        check_vma=False,
    )
```

```python
import functools

import jax
import jax.numpy as jnp
from jax import lax
from jax.experimental import pallas as pl
from jax.experimental.pallas import tpu as pltpu
from jax.sharding import PartitionSpec as P

ROUTED_SCALE = 2.5
MIB = 1024 * 1024


def shift(value, axis, by):
    size = lax.axis_size(axis)
    return lax.ppermute(value, axis, [(i, (i + by) % size) for i in range(size)])


def shift_expert(value, by_expert, by_tp=0):
    groups, n_tp = lax.axis_size("grp"), lax.axis_size("tp")
    pairs = []
    for g in range(groups):
        for t in range(n_tp):
            to = (g + 2 * by_expert) % groups * n_tp + (t + by_tp) % n_tp
            pairs.append((g * n_tp + t, to))
    return lax.ppermute(value, ("grp", "tp"), pairs)


def swap_half(value):
    return lax.ppermute(value, "grp", [(i, i ^ 1) for i in range(lax.axis_size("grp"))])


def hand_on(*refs):
    del refs


def after(value, *earlier, flops=0):
    return pl.pallas_call(
        hand_on,
        out_shape=jax.ShapeDtypeStruct(value.shape, value.dtype),
        in_specs=[pl.BlockSpec(memory_space=pl.ANY)] * (1 + len(earlier)),
        out_specs=pl.BlockSpec(memory_space=pl.ANY),
        input_output_aliases={0: 0},
        cost_estimate=pl.CostEstimate(flops=flops, bytes_accessed=0, transcendentals=0),
        compiler_params=pltpu.CompilerParams(vmem_limit_bytes=MIB),
    )(value, *earlier)


def copy_kernel(from_ref, to_ref):
    to_ref[...] = from_ref[...]


def copied(value):
    return pl.pallas_call(
        copy_kernel,
        out_shape=jax.ShapeDtypeStruct(value.shape, value.dtype),
        compiler_params=pltpu.CompilerParams(vmem_limit_bytes=2 * MIB),
    )(value)


def mix_kernel(n_tp, experts, ids_ref, levels_ref, *refs):
    *piece_refs, mixed_ref = refs
    count = mixed_ref.shape[0]
    expert = lax.axis_index("grp") // 2
    row = lax.broadcasted_iota(jnp.int32, (count, count), 0)
    column = lax.broadcasted_iota(jnp.int32, (count, count), 1)
    ids = ids_ref[...]
    levels = levels_ref[...].astype(jnp.float32)
    whole = jnp.sum(levels, axis=0, keepdims=True)
    mixed = jnp.zeros(mixed_ref.shape, jnp.float32)
    for s in range(experts):
        source = lax.rem(expert - s + experts, experts)
        weight = ROUTED_SCALE * jnp.sum(jnp.where(ids == source, levels, 0.0), axis=0, keepdims=True) / whole
        upright = jnp.sum(jnp.where(row == column, weight, 0.0), axis=1, keepdims=True)
        total = piece_refs[s * n_tp][...].astype(jnp.float32)
        for t in range(1, n_tp):
            total = total + piece_refs[s * n_tp + t][...].astype(jnp.float32)
        mixed = mixed + upright * total.astype(jnp.bfloat16).astype(jnp.float32)
    mixed_ref[...] = mixed.astype(mixed_ref.dtype)


def mix(expert_ids, gate_levels, pieces, n_tp, experts):
    return pl.pallas_call(
        functools.partial(mix_kernel, n_tp, experts),
        out_shape=jax.ShapeDtypeStruct(pieces[0].shape, jnp.bfloat16),
        compiler_params=pltpu.CompilerParams(vmem_limit_bytes=12 * MIB),
    )(expert_ids.T, gate_levels.T, *pieces)


def per_device(tokens, expert_ids, gate_levels, gate_weight, up_weight, down_weight):
    bf16, f32 = jnp.bfloat16, jnp.float32
    experts = lax.axis_size("grp") // 2
    n_tp, n_ex = lax.axis_size("tp"), lax.axis_size("ex")
    count, width = tokens.shape
    w_gate, w_up, w_down = gate_weight[0], up_weight[0], down_weight[0]
    inner = w_down.shape[0]

    def partial_sums(rows):
        parts = [jnp.dot(rows, w, preferred_element_type=f32) for w in (w_gate, w_up)]
        part = jnp.concatenate(parts, axis=1)
        sent = part.astype(bf16)
        return part, sent, [shift(sent, "ex", s) for s in range(1, n_ex)]

    def partial_out(part, others, kept_flops, part_flops=0, *earlier):
        if part_flops:
            part = after(part, flops=part_flops)
        for other in others:
            part = part + other.astype(f32)
        hidden = (jax.nn.silu(part[:, :inner]) * part[:, inner:]).astype(bf16)
        out = jnp.dot(hidden, w_down, preferred_element_type=f32)
        kept = out.shape[0] // 2
        swapped = swap_half(out[kept:].astype(bf16)).astype(f32)
        if kept_flops:
            out = after(after(out, *earlier) if earlier else out, flops=kept_flops)
        return out[:kept] + swapped

    held = copied(tokens)
    places = (0, n_tp - 1, *range(1, n_tp - 1))
    blocks = [held] + [shift(tokens, "tp", t) for t in places[1:]]
    straight = n_tp // 2
    far = [[shift_expert(tokens, s, t) if t == straight else shift_expert(rows, s) for t, rows in zip(places, blocks)] for s in range(1, experts)]
    near = jnp.concatenate(blocks, axis=0)
    near_swapped = swap_half(after(near, *(line[places.index(1)] for line in far)))
    near = jnp.concatenate([near, near_swapped], axis=0)
    near_part, near_sent, near_others = partial_sums(near)
    far = [after(rows, near_sent) if i > 1 else rows for line in far for i, rows in enumerate(line)]
    far = jnp.concatenate(far, axis=0)
    far_swapped = swap_half(far)
    far = jnp.concatenate([after(far, flops=3450000000), far_swapped], axis=0)
    far_part, far_sent, far_others = partial_sums(far)
    near_out = partial_out(near_part, [after(other, far_sent) for other in near_others], 3450000000, 3450000000)
    near_out = near_out.reshape(n_tp, count, width)
    near_sent = near_out[1:].astype(bf16)
    pieces = [near_out[0]] + [shift(near_sent[i], "tp", -t) for i, t in enumerate(places[1:])]
    far_out = partial_out(far_part, [after(other, near_sent) for other in far_others], 0, 0)
    far_out = far_out.reshape(experts - 1, n_tp, count, width).astype(bf16)
    for s in range(1, experts):
        pieces += [shift_expert(far_out[experts - 1 - s, i], s, -t) for i, t in enumerate(places)]
    return mix(expert_ids, gate_levels, pieces, n_tp, experts)


def solution(mesh):
    return jax.shard_map(
        per_device,
        mesh=mesh,
        in_specs=(
            P(("grp", "tp"), "ex"),
            P(("grp", "tp"), None),
            P(("grp", "tp"), None),
            P("grp", "ex", "tp"),
            P("grp", "ex", "tp"),
            P("grp", "tp", "ex"),
        ),
        out_specs=P(("grp", "tp"), "ex"),
        check_vma=False,
    )
```

```python
import functools

import jax
import jax.numpy as jnp
from jax import lax
from jax.experimental import pallas as pl
from jax.experimental.pallas import tpu as pltpu
from jax.sharding import PartitionSpec as P

ROUTED_SCALE = 2.5
MIB = 1024 * 1024


def rotate(value, axis, by):
    size = lax.axis_size(axis)
    return lax.ppermute(value, axis, [(i, (i + by) % size) for i in range(size)])


def rotate_experts(value, by):
    groups = lax.axis_size("grp")
    return lax.ppermute(value, "grp", [(i, (i + 2 * by) % groups) for i in range(groups)])


def partner(place, step, size):
    return place ^ abs(step) if size & (size - 1) == 0 else (place + step) % size


def exchange(value, by_expert, step):
    groups, n_tp = lax.axis_size("grp"), lax.axis_size("tp")
    pairs = []
    for g in range(groups):
        for t in range(n_tp):
            to = (g + 2 * by_expert) % groups * n_tp + partner(t, step, n_tp)
            pairs.append((g * n_tp + t, to))
    return lax.ppermute(value, ("grp", "tp"), pairs)


def swap_half(value):
    return lax.ppermute(value, "grp", [(i, i ^ 1) for i in range(lax.axis_size("grp"))])


def hand_on(*refs):
    del refs


def after(value, *earlier, flops=0):
    return pl.pallas_call(
        hand_on,
        out_shape=jax.ShapeDtypeStruct(value.shape, value.dtype),
        in_specs=[pl.BlockSpec(memory_space=pl.ANY)] * (1 + len(earlier)),
        out_specs=pl.BlockSpec(memory_space=pl.ANY),
        input_output_aliases={0: 0},
        cost_estimate=pl.CostEstimate(flops=flops, bytes_accessed=0, transcendentals=0),
        compiler_params=pltpu.CompilerParams(vmem_limit_bytes=MIB),
    )(value, *earlier)


def copy_kernel(from_ref, to_ref):
    to_ref[...] = from_ref[...]


def copied(value):
    return pl.pallas_call(
        copy_kernel,
        out_shape=jax.ShapeDtypeStruct(value.shape, value.dtype),
        compiler_params=pltpu.CompilerParams(vmem_limit_bytes=2 * MIB),
    )(value)


def mix_kernel(n_tp, experts, ids_ref, levels_ref, *refs):
    *piece_refs, mixed_ref = refs
    count = mixed_ref.shape[0]
    expert = lax.axis_index("grp") // 2
    row = lax.broadcasted_iota(jnp.int32, (count, count), 0)
    column = lax.broadcasted_iota(jnp.int32, (count, count), 1)
    ids = ids_ref[...]
    levels = levels_ref[...].astype(jnp.float32)
    whole = jnp.sum(levels, axis=0, keepdims=True)
    mixed = jnp.zeros(mixed_ref.shape, jnp.float32)
    for s in range(experts):
        source = lax.rem(expert - s + experts, experts)
        weight = ROUTED_SCALE * jnp.sum(jnp.where(ids == source, levels, 0.0), axis=0, keepdims=True) / whole
        upright = jnp.sum(jnp.where(row == column, weight, 0.0), axis=1, keepdims=True)
        total = piece_refs[s * n_tp][...].astype(jnp.float32)
        for t in range(1, n_tp):
            total = total + piece_refs[s * n_tp + t][...].astype(jnp.float32)
        mixed = mixed + upright * total.astype(jnp.bfloat16).astype(jnp.float32)
    mixed_ref[...] = mixed.astype(mixed_ref.dtype)


def mix(expert_ids, gate_levels, pieces, n_tp, experts):
    return pl.pallas_call(
        functools.partial(mix_kernel, n_tp, experts),
        out_shape=jax.ShapeDtypeStruct(pieces[0].shape, jnp.bfloat16),
        compiler_params=pltpu.CompilerParams(vmem_limit_bytes=12 * MIB),
    )(expert_ids.T, gate_levels.T, *pieces)


def per_device(tokens, expert_ids, gate_levels, gate_weight, up_weight, down_weight):
    bf16, f32 = jnp.bfloat16, jnp.float32
    experts = lax.axis_size("grp") // 2
    n_tp, n_ex = lax.axis_size("tp"), lax.axis_size("ex")
    count, width = tokens.shape
    w_gate, w_up, w_down = gate_weight[0], up_weight[0], down_weight[0]
    inner = w_down.shape[0]

    def partial_sums(rows):
        parts = [jnp.dot(rows, w, preferred_element_type=f32) for w in (w_gate, w_up)]
        part = jnp.concatenate(parts, axis=1)
        sent = part.astype(bf16)
        return part, sent, [rotate(sent, "ex", s) for s in range(1, n_ex)]

    def partial_out(part, others, kept_flops, part_flops=0, *earlier):
        if part_flops:
            part = after(part, flops=part_flops)
        for other in others:
            part = part + other.astype(f32)
        hidden = (jax.nn.silu(part[:, :inner]) * part[:, inner:]).astype(bf16)
        out = jnp.dot(hidden, w_down, preferred_element_type=f32)
        kept = out.shape[0] // 2
        swapped = swap_half(out[kept:].astype(bf16)).astype(f32)
        if kept_flops:
            out = after(after(out, *earlier) if earlier else out, flops=kept_flops)
        return out[:kept] + swapped

    held = copied(tokens)
    places = tuple(range(n_tp))
    blocks = [held] + [exchange(tokens, 0, t) for t in places[1:]]
    far = [[rotate_experts(rows, s) for rows in blocks] for s in range(1, experts)]
    near = jnp.concatenate(blocks, axis=0)
    near_swapped = swap_half(after(near, *(line[1] for line in far)))
    near = jnp.concatenate([near, near_swapped], axis=0)
    near_part, near_sent, near_others = partial_sums(near)
    far = [after(rows, near_sent) if i == n_tp - 1 else rows for line in far for i, rows in enumerate(line)]
    far = jnp.concatenate(far, axis=0)
    far_swapped = swap_half(far)
    far = jnp.concatenate([after(far, flops=3450000000), far_swapped], axis=0)
    far_part, far_sent, far_others = partial_sums(far)
    near_out = partial_out(near_part, [after(other, far_sent) for other in near_others], 3450000000, 0)
    near_out = near_out.reshape(n_tp, count, width)
    near_sent = near_out[1:].astype(bf16)
    pieces = [near_out[0]] + [exchange(near_sent[i], 0, -t) for i, t in enumerate(places[1:])]
    far_out = partial_out(far_part, [after(other, near_sent) for other in far_others], 0, 0)
    far_out = far_out.reshape(experts - 1, n_tp, count, width).astype(bf16)
    for s in range(1, experts):
        pieces += [exchange(far_out[experts - 1 - s, i], s, -t) for i, t in enumerate(places)]
    return mix(expert_ids, gate_levels, pieces, n_tp, experts)


def solution(mesh):
    return jax.shard_map(
        per_device,
        mesh=mesh,
        in_specs=(
            P(("grp", "tp"), "ex"),
            P(("grp", "tp"), None),
            P(("grp", "tp"), None),
            P("grp", "ex", "tp"),
            P("grp", "ex", "tp"),
            P("grp", "tp", "ex"),
        ),
        out_specs=P(("grp", "tp"), "ex"),
        check_vma=False,
    )
```

```python
import functools

import jax
import jax.numpy as jnp
from jax import lax
from jax.experimental import pallas as pl
from jax.experimental.pallas import tpu as pltpu
from jax.sharding import PartitionSpec as P

ROUTED_SCALE = 2.5
MIB = 1024 * 1024


def rotate(value, axis, by):
    size = lax.axis_size(axis)
    return lax.ppermute(value, axis, [(i, (i + by) % size) for i in range(size)])


def rotate_experts(value, by):
    groups = lax.axis_size("grp")
    return lax.ppermute(value, "grp", [(i, (i + 2 * by) % groups) for i in range(groups)])


def partner(place, step, size):
    return place ^ abs(step) if size & (size - 1) == 0 else (place + step) % size


def exchange(value, by_expert, step):
    groups, n_tp = lax.axis_size("grp"), lax.axis_size("tp")
    pairs = []
    for g in range(groups):
        for t in range(n_tp):
            to = (g + 2 * by_expert) % groups * n_tp + partner(t, step, n_tp)
            pairs.append((g * n_tp + t, to))
    return lax.ppermute(value, ("grp", "tp"), pairs)


def swap_half(value):
    return lax.ppermute(value, "grp", [(i, i ^ 1) for i in range(lax.axis_size("grp"))])


def hand_on(*refs):
    del refs


def after(value, *earlier, flops=0):
    return pl.pallas_call(
        hand_on,
        out_shape=jax.ShapeDtypeStruct(value.shape, value.dtype),
        in_specs=[pl.BlockSpec(memory_space=pl.ANY)] * (1 + len(earlier)),
        out_specs=pl.BlockSpec(memory_space=pl.ANY),
        input_output_aliases={0: 0},
        cost_estimate=pl.CostEstimate(flops=flops, bytes_accessed=0, transcendentals=0),
        compiler_params=pltpu.CompilerParams(vmem_limit_bytes=MIB),
    )(value, *earlier)


def copy_kernel(from_ref, to_ref):
    to_ref[...] = from_ref[...]


def copied(value):
    return pl.pallas_call(
        copy_kernel,
        out_shape=jax.ShapeDtypeStruct(value.shape, value.dtype),
        compiler_params=pltpu.CompilerParams(vmem_limit_bytes=2 * MIB),
    )(value)


def mix_kernel(n_tp, experts, ids_ref, levels_ref, *refs):
    *piece_refs, mixed_ref = refs
    count = mixed_ref.shape[0]
    expert = lax.axis_index("grp") // 2
    row = lax.broadcasted_iota(jnp.int32, (count, count), 0)
    column = lax.broadcasted_iota(jnp.int32, (count, count), 1)
    ids = ids_ref[...]
    levels = levels_ref[...].astype(jnp.float32)
    whole = jnp.sum(levels, axis=0, keepdims=True)
    mixed = jnp.zeros(mixed_ref.shape, jnp.float32)
    for s in range(experts):
        source = lax.rem(expert - s + experts, experts)
        weight = ROUTED_SCALE * jnp.sum(jnp.where(ids == source, levels, 0.0), axis=0, keepdims=True) / whole
        upright = jnp.sum(jnp.where(row == column, weight, 0.0), axis=1, keepdims=True)
        total = piece_refs[s * n_tp][...].astype(jnp.float32)
        for t in range(1, n_tp):
            total = total + piece_refs[s * n_tp + t][...].astype(jnp.float32)
        mixed = mixed + upright * total.astype(jnp.bfloat16).astype(jnp.float32)
    mixed_ref[...] = mixed.astype(mixed_ref.dtype)


def mix(expert_ids, gate_levels, pieces, n_tp, experts):
    return pl.pallas_call(
        functools.partial(mix_kernel, n_tp, experts),
        out_shape=jax.ShapeDtypeStruct(pieces[0].shape, jnp.bfloat16),
        compiler_params=pltpu.CompilerParams(vmem_limit_bytes=12 * MIB),
    )(expert_ids.T, gate_levels.T, *pieces)


def per_device(tokens, expert_ids, gate_levels, gate_weight, up_weight, down_weight):
    bf16, f32 = jnp.bfloat16, jnp.float32
    experts = lax.axis_size("grp") // 2
    n_tp, n_ex = lax.axis_size("tp"), lax.axis_size("ex")
    count, width = tokens.shape
    w_gate, w_up, w_down = gate_weight[0], up_weight[0], down_weight[0]
    inner = w_down.shape[0]

    def partial_sums(rows):
        parts = [jnp.dot(rows, w, preferred_element_type=f32) for w in (w_gate, w_up)]
        part = jnp.concatenate(parts, axis=1)
        sent = part.astype(bf16)
        return part, sent, [rotate(sent, "ex", s) for s in range(1, n_ex)]

    def partial_out(part, others, kept_flops, part_flops=0, *earlier):
        if part_flops:
            part = after(part, flops=part_flops)
        for other in others:
            part = part + other.astype(f32)
        hidden = (jax.nn.silu(part[:, :inner]) * part[:, inner:]).astype(bf16)
        out = jnp.dot(hidden, w_down, preferred_element_type=f32)
        kept = out.shape[0] // 2
        swapped = swap_half(out[kept:].astype(bf16)).astype(f32)
        if kept_flops:
            out = after(after(out, *earlier) if earlier else out, flops=kept_flops)
        return out[:kept] + swapped

    held = copied(tokens)
    places = tuple(range(n_tp))
    blocks = [held] + [exchange(tokens, 0, t) for t in places[1:]]
    far = [[rotate_experts(rows, s) for rows in blocks] for s in range(1, experts)]
    near = jnp.concatenate(blocks, axis=0)
    near_swapped = swap_half(after(near, *(line[1] for line in far)))
    near = jnp.concatenate([near, near_swapped], axis=0)
    near_part, near_sent, near_others = partial_sums(near)
    far = [after(rows, near_sent) if i == n_tp - 1 else rows for line in far for i, rows in enumerate(line)]
    far = jnp.concatenate(far, axis=0)
    far_swapped = swap_half(far)
    far = jnp.concatenate([after(far, flops=3450000000), far_swapped], axis=0)
    far_part, far_sent, far_others = partial_sums(far)
    near_out = partial_out(near_part, [after(other, far_sent) for other in near_others], 3450000000, 3450000000)
    near_out = near_out.reshape(n_tp, count, width)
    near_sent = near_out[1:].astype(bf16)
    pieces = [near_out[0]] + [exchange(near_sent[i], 0, -t) for i, t in enumerate(places[1:])]
    far_out = partial_out(far_part, [after(other, near_sent) for other in far_others], 0, 0)
    far_out = far_out.reshape(experts - 1, n_tp, count, width).astype(bf16)
    for s in range(1, experts):
        pieces += [exchange(far_out[experts - 1 - s, i], s, -t) for i, t in enumerate(places)]
    return mix(expert_ids, gate_levels, pieces, n_tp, experts)


def solution(mesh):
    return jax.shard_map(
        per_device,
        mesh=mesh,
        in_specs=(
            P(("grp", "tp"), "ex"),
            P(("grp", "tp"), None),
            P(("grp", "tp"), None),
            P("grp", "ex", "tp"),
            P("grp", "ex", "tp"),
            P("grp", "tp", "ex"),
        ),
        out_specs=P(("grp", "tp"), "ex"),
        check_vma=False,
    )
```

```python
import functools

import jax
import jax.numpy as jnp
from jax import lax
from jax.experimental import pallas as pl
from jax.experimental.pallas import tpu as pltpu
from jax.sharding import PartitionSpec as P

ROUTED_SCALE = 2.5
MIB = 1024 * 1024


def rotate(value, axis, by):
    size = lax.axis_size(axis)
    return lax.ppermute(value, axis, [(i, (i + by) % size) for i in range(size)])


def rotate_experts(value, by):
    groups = lax.axis_size("grp")
    return lax.ppermute(value, "grp", [(i, (i + 2 * by) % groups) for i in range(groups)])


def partner(place, step, size):
    return place ^ abs(step) if size & (size - 1) == 0 else (place + step) % size


def exchange(value, by_expert, step):
    groups, n_tp = lax.axis_size("grp"), lax.axis_size("tp")
    pairs = []
    for g in range(groups):
        for t in range(n_tp):
            to = (g + 2 * by_expert) % groups * n_tp + partner(t, step, n_tp)
            pairs.append((g * n_tp + t, to))
    return lax.ppermute(value, ("grp", "tp"), pairs)


def swap_half(value):
    return lax.ppermute(value, "grp", [(i, i ^ 1) for i in range(lax.axis_size("grp"))])


def hand_on(*refs):
    del refs


def after(value, *earlier, flops=0):
    return pl.pallas_call(
        hand_on,
        out_shape=jax.ShapeDtypeStruct(value.shape, value.dtype),
        in_specs=[pl.BlockSpec(memory_space=pl.ANY)] * (1 + len(earlier)),
        out_specs=pl.BlockSpec(memory_space=pl.ANY),
        input_output_aliases={0: 0},
        cost_estimate=pl.CostEstimate(flops=flops, bytes_accessed=0, transcendentals=0),
        compiler_params=pltpu.CompilerParams(vmem_limit_bytes=MIB),
    )(value, *earlier)


def copy_kernel(from_ref, to_ref):
    to_ref[...] = from_ref[...]


def copied(value):
    return pl.pallas_call(
        copy_kernel,
        out_shape=jax.ShapeDtypeStruct(value.shape, value.dtype),
        compiler_params=pltpu.CompilerParams(vmem_limit_bytes=2 * MIB),
    )(value)


def in_line_order(pieces, n_tp):
    lines = [pieces[i : i + n_tp] for i in range(0, len(pieces), n_tp)]
    return [piece for line in lines for piece in (line[0], *line[:0:-1])]


def mix_kernel(n_tp, experts, ids_ref, levels_ref, *refs):
    *piece_refs, mixed_ref = refs
    piece_refs = in_line_order(piece_refs, n_tp)
    count = mixed_ref.shape[0]
    expert = lax.axis_index("grp") // 2
    row = lax.broadcasted_iota(jnp.int32, (count, count), 0)
    column = lax.broadcasted_iota(jnp.int32, (count, count), 1)
    ids = ids_ref[...]
    levels = levels_ref[...].astype(jnp.float32)
    whole = jnp.sum(levels, axis=0, keepdims=True)
    mixed = jnp.zeros(mixed_ref.shape, jnp.float32)
    for s in range(experts):
        source = lax.rem(expert - s + experts, experts)
        weight = ROUTED_SCALE * jnp.sum(jnp.where(ids == source, levels, 0.0), axis=0, keepdims=True) / whole
        upright = jnp.sum(jnp.where(row == column, weight, 0.0), axis=1, keepdims=True)
        total = piece_refs[s * n_tp][...].astype(jnp.float32)
        for t in range(1, n_tp):
            total = total + piece_refs[s * n_tp + t][...].astype(jnp.float32)
        mixed = mixed + upright * total.astype(jnp.bfloat16).astype(jnp.float32)
    mixed_ref[...] = mixed.astype(mixed_ref.dtype)


def mix(expert_ids, gate_levels, pieces, n_tp, experts):
    return pl.pallas_call(
        functools.partial(mix_kernel, n_tp, experts),
        out_shape=jax.ShapeDtypeStruct(pieces[0].shape, jnp.bfloat16),
        compiler_params=pltpu.CompilerParams(vmem_limit_bytes=12 * MIB),
    )(expert_ids.T, gate_levels.T, *pieces)


def per_device(tokens, expert_ids, gate_levels, gate_weight, up_weight, down_weight):
    bf16, f32 = jnp.bfloat16, jnp.float32
    experts = lax.axis_size("grp") // 2
    n_tp, n_ex = lax.axis_size("tp"), lax.axis_size("ex")
    count, width = tokens.shape
    w_gate, w_up, w_down = gate_weight[0], up_weight[0], down_weight[0]
    inner = w_down.shape[0]

    def partial_sums(rows):
        parts = [jnp.dot(rows, w, preferred_element_type=f32) for w in (w_gate, w_up)]
        part = jnp.concatenate(parts, axis=1)
        sent = part.astype(bf16)
        return part, sent, [rotate(sent, "ex", s) for s in range(1, n_ex)]

    def partial_out(part, others, kept_flops, part_flops=0, *earlier):
        if part_flops:
            part = after(part, flops=part_flops)
        for other in others:
            part = part + other.astype(f32)
        hidden = (jax.nn.silu(part[:, :inner]) * part[:, inner:]).astype(bf16)
        out = jnp.dot(hidden, w_down, preferred_element_type=f32)
        kept = out.shape[0] // 2
        swapped = swap_half(out[kept:].astype(bf16)).astype(f32)
        if kept_flops:
            out = after(after(out, *earlier) if earlier else out, flops=kept_flops)
        return out[:kept] + swapped

    held = copied(tokens)
    places = tuple(range(n_tp))
    blocks = [held] + [exchange(tokens, 0, t) for t in places[1:]]
    far = [[rotate_experts(rows, s) for rows in blocks] for s in range(1, experts)]
    near = jnp.concatenate(blocks, axis=0)
    near_swapped = swap_half(after(near, *(line[1] for line in far)))
    near = jnp.concatenate([near, near_swapped], axis=0)
    near_part, near_sent, near_others = partial_sums(near)
    far = [after(rows, near_sent) if i == n_tp - 1 else rows for line in far for i, rows in enumerate(line)]
    far = jnp.concatenate(far, axis=0)
    far_swapped = swap_half(far)
    far = jnp.concatenate([after(far, flops=3450000000), far_swapped], axis=0)
    far_part, far_sent, far_others = partial_sums(far)
    near_out = partial_out(near_part, [after(other, far_sent) for other in near_others], 3450000000, 0)
    near_out = near_out.reshape(n_tp, count, width)
    near_sent = near_out[1:].astype(bf16)
    pieces = [near_out[0]] + [exchange(near_sent[i], 0, -t) for i, t in enumerate(places[1:])]
    far_out = partial_out(far_part, [after(other, near_sent) for other in far_others], 0, 0)
    far_out = far_out.reshape(experts - 1, n_tp, count, width).astype(bf16)
    for s in range(1, experts):
        pieces += [exchange(far_out[experts - 1 - s, i], s, -t) for i, t in enumerate(places)]
    return mix(expert_ids, gate_levels, in_line_order(pieces, n_tp), n_tp, experts)


def solution(mesh):
    return jax.shard_map(
        per_device,
        mesh=mesh,
        in_specs=(
            P(("grp", "tp"), "ex"),
            P(("grp", "tp"), None),
            P(("grp", "tp"), None),
            P("grp", "ex", "tp"),
            P("grp", "ex", "tp"),
            P("grp", "tp", "ex"),
        ),
        out_specs=P(("grp", "tp"), "ex"),
        check_vma=False,
    )
```

```python
import functools

import jax
import jax.numpy as jnp
from jax import lax
from jax.experimental import pallas as pl
from jax.experimental.pallas import tpu as pltpu
from jax.sharding import PartitionSpec as P

ROUTED_SCALE = 2.5
MIB = 1024 * 1024


def rotate(value, axis, by):
    size = lax.axis_size(axis)
    return lax.ppermute(value, axis, [(i, (i + by) % size) for i in range(size)])


def rotate_experts(value, by):
    groups = lax.axis_size("grp")
    return lax.ppermute(value, "grp", [(i, (i + 2 * by) % groups) for i in range(groups)])


def partner(place, step, size):
    return place ^ abs(step) if size & (size - 1) == 0 else (place + step) % size


def exchange(value, by_expert, *steps):
    groups, n_tp = lax.axis_size("grp"), lax.axis_size("tp")
    pairs = []
    for g in range(groups):
        for t in range(n_tp):
            to = (g + 2 * by_expert) % groups * n_tp + partner(t, steps[g % len(steps)], n_tp)
            pairs.append((g * n_tp + t, to))
    return lax.ppermute(value, ("grp", "tp"), pairs)


def swap_half(value):
    return lax.ppermute(value, "grp", [(i, i ^ 1) for i in range(lax.axis_size("grp"))])


def hand_on(*refs):
    del refs


def after(value, *earlier, flops=0):
    return pl.pallas_call(
        hand_on,
        out_shape=jax.ShapeDtypeStruct(value.shape, value.dtype),
        in_specs=[pl.BlockSpec(memory_space=pl.ANY)] * (1 + len(earlier)),
        out_specs=pl.BlockSpec(memory_space=pl.ANY),
        input_output_aliases={0: 0},
        cost_estimate=pl.CostEstimate(flops=flops, bytes_accessed=0, transcendentals=0),
        compiler_params=pltpu.CompilerParams(vmem_limit_bytes=MIB),
    )(value, *earlier)


def copy_kernel(from_ref, to_ref):
    to_ref[...] = from_ref[...]


def copied(value):
    return pl.pallas_call(
        copy_kernel,
        out_shape=jax.ShapeDtypeStruct(value.shape, value.dtype),
        compiler_params=pltpu.CompilerParams(vmem_limit_bytes=2 * MIB),
    )(value)


def mix_kernel(n_tp, experts, ids_ref, levels_ref, *refs):
    *piece_refs, mixed_ref = refs
    count = mixed_ref.shape[0]
    expert = lax.axis_index("grp") // 2
    row = lax.broadcasted_iota(jnp.int32, (count, count), 0)
    column = lax.broadcasted_iota(jnp.int32, (count, count), 1)
    ids = ids_ref[...]
    levels = levels_ref[...].astype(jnp.float32)
    whole = jnp.sum(levels, axis=0, keepdims=True)
    mixed = jnp.zeros(mixed_ref.shape, jnp.float32)
    for s in range(experts):
        source = lax.rem(expert - s + experts, experts)
        weight = ROUTED_SCALE * jnp.sum(jnp.where(ids == source, levels, 0.0), axis=0, keepdims=True) / whole
        upright = jnp.sum(jnp.where(row == column, weight, 0.0), axis=1, keepdims=True)
        total = piece_refs[s * n_tp][...].astype(jnp.float32)
        for t in range(1, n_tp):
            total = total + piece_refs[s * n_tp + t][...].astype(jnp.float32)
        mixed = mixed + upright * total.astype(jnp.bfloat16).astype(jnp.float32)
    mixed_ref[...] = mixed.astype(mixed_ref.dtype)


def mix(expert_ids, gate_levels, pieces, n_tp, experts):
    return pl.pallas_call(
        functools.partial(mix_kernel, n_tp, experts),
        out_shape=jax.ShapeDtypeStruct(pieces[0].shape, jnp.bfloat16),
        compiler_params=pltpu.CompilerParams(vmem_limit_bytes=12 * MIB),
    )(expert_ids.T, gate_levels.T, *pieces)


def per_device(tokens, expert_ids, gate_levels, gate_weight, up_weight, down_weight):
    bf16, f32 = jnp.bfloat16, jnp.float32
    experts = lax.axis_size("grp") // 2
    n_tp, n_ex = lax.axis_size("tp"), lax.axis_size("ex")
    count, width = tokens.shape
    w_gate, w_up, w_down = gate_weight[0], up_weight[0], down_weight[0]
    inner = w_down.shape[0]

    def partial_sums(rows):
        parts = [jnp.dot(rows, w, preferred_element_type=f32) for w in (w_gate, w_up)]
        part = jnp.concatenate(parts, axis=1)
        sent = part.astype(bf16)
        return part, sent, [rotate(sent, "ex", s) for s in range(1, n_ex)]

    def partial_out(part, others, kept_flops, part_flops=0, *earlier):
        if part_flops:
            part = after(part, flops=part_flops)
        for other in others:
            part = part + other.astype(f32)
        hidden = (jax.nn.silu(part[:, :inner]) * part[:, inner:]).astype(bf16)
        out = jnp.dot(hidden, w_down, preferred_element_type=f32)
        out = out.reshape(2, -1, n_tp, count, width)
        kept, sent = [], []
        for line in range(out.shape[1]):
            own, other = out[0, line], out[1, line]
            for t in (0, half):
                kept.append(own[places.index(t)])
                sent.append(other[places.index(t)])
            for t in range(1, half):
                low, high = places.index(t), places.index(n_tp - t)
                for mine, theirs in ((own, other), (other, own)):
                    kept.append(jnp.where(odd, mine[high], mine[low]))
                    sent.append(jnp.where(odd, theirs[low], theirs[high]))
        swapped = swap_half(jnp.concatenate(sent, axis=0).astype(bf16)).astype(f32)
        kept = jnp.concatenate(kept, axis=0)
        if kept_flops:
            kept = after(kept, flops=kept_flops)
        return (kept + swapped).reshape(-1, n_tp * count, width)

    def send_back(rows, by_expert):
        rows = rows.astype(bf16)
        pieces = [exchange(rows[2 * i * count : 2 * (i + 1) * count], by_expert, -i, i - n_tp) for i in range(1, half)]
        pieces.append(exchange(rows[count : 2 * count], by_expert, -half))
        if by_expert:
            pieces.append(exchange(rows[:count], by_expert, 0))
        return pieces

    half = n_tp // 2
    odd = lax.axis_index("grp") % 2 == 1
    places = tuple(range(n_tp))
    held = copied(tokens)
    blocks = [held] + [exchange(tokens, 0, t) for t in places[1:]]
    far = [[rotate_experts(rows, s) for rows in blocks] for s in range(1, experts)]
    near = jnp.concatenate(blocks, axis=0)
    near_swapped = swap_half(after(near, *(line[1] for line in far)))
    near = jnp.concatenate([near, near_swapped], axis=0)
    near_part, near_sent, near_others = partial_sums(near)
    far = [after(rows, near_sent) if i == n_tp - 1 else rows for line in far for i, rows in enumerate(line)]
    far = jnp.concatenate(far, axis=0)
    far_swapped = swap_half(far)
    far = jnp.concatenate([after(far, flops=3450000000), far_swapped], axis=0)
    far_part, far_sent, far_others = partial_sums(far)
    near_out = partial_out(near_part, [after(other, far_sent) for other in near_others], 3450000000, 0)
    backs = [send_back(near_out[0], 0)]
    far_out = partial_out(far_part, [after(other, near_out) for other in far_others], 0, 0)
    backs += [send_back(far_out[experts - 1 - s], s) for s in range(1, experts)]
    late = [piece for back in backs[1:] for piece in back]
    backs[0] = [after(piece, *late) for piece in backs[0]]
    pairs = [back[i] for back in backs for i in range(half - 1)]
    handed = jnp.concatenate([pair[count:] for pair in pairs], axis=0)
    handed = swap_half(after(handed, *(piece for back in backs[1:] for piece in back[half - 1 :])))
    handed = handed.reshape(experts, half - 1, count, width)
    pieces = []
    for s, back in enumerate(backs):
        pieces += [back[half] if s else near_out[0, :count], back[half - 1]]
        for i in range(half - 1):
            pieces += [back[i][:count], handed[s, i]]
    return mix(expert_ids, gate_levels, pieces, n_tp, experts)


def solution(mesh):
    return jax.shard_map(
        per_device,
        mesh=mesh,
        in_specs=(
            P(("grp", "tp"), "ex"),
            P(("grp", "tp"), None),
            P(("grp", "tp"), None),
            P("grp", "ex", "tp"),
            P("grp", "ex", "tp"),
            P("grp", "tp", "ex"),
        ),
        out_specs=P(("grp", "tp"), "ex"),
        check_vma=False,
    )
```

```python
import functools

import jax
import jax.numpy as jnp
from jax import lax
from jax.experimental import pallas as pl
from jax.experimental.pallas import tpu as pltpu
from jax.sharding import PartitionSpec as P

ROUTED_SCALE = 2.5
MIB = 1024 * 1024


def rotate(value, axis, by):
    size = lax.axis_size(axis)
    return lax.ppermute(value, axis, [(i, (i + by) % size) for i in range(size)])


def rotate_experts(value, by):
    groups = lax.axis_size("grp")
    return lax.ppermute(value, "grp", [(i, (i + 2 * by) % groups) for i in range(groups)])


def partner(place, step, size):
    return place ^ abs(step) if size & (size - 1) == 0 else (place + step) % size


def exchange(value, by_expert, *steps):
    groups, n_tp = lax.axis_size("grp"), lax.axis_size("tp")
    pairs = []
    for g in range(groups):
        for t in range(n_tp):
            to = (g + 2 * by_expert) % groups * n_tp + partner(t, steps[g % len(steps)], n_tp)
            pairs.append((g * n_tp + t, to))
    return lax.ppermute(value, ("grp", "tp"), pairs)


def swap_half(value):
    return lax.ppermute(value, "grp", [(i, i ^ 1) for i in range(lax.axis_size("grp"))])


def hand_on(*refs):
    del refs


def after(value, *earlier, flops=0):
    return pl.pallas_call(
        hand_on,
        out_shape=jax.ShapeDtypeStruct(value.shape, value.dtype),
        in_specs=[pl.BlockSpec(memory_space=pl.ANY)] * (1 + len(earlier)),
        out_specs=pl.BlockSpec(memory_space=pl.ANY),
        input_output_aliases={0: 0},
        cost_estimate=pl.CostEstimate(flops=flops, bytes_accessed=0, transcendentals=0),
        compiler_params=pltpu.CompilerParams(vmem_limit_bytes=MIB),
    )(value, *earlier)


def copy_kernel(from_ref, to_ref):
    to_ref[...] = from_ref[...]


def copied(value):
    return pl.pallas_call(
        copy_kernel,
        out_shape=jax.ShapeDtypeStruct(value.shape, value.dtype),
        compiler_params=pltpu.CompilerParams(vmem_limit_bytes=2 * MIB),
    )(value)


def mix_kernel(n_tp, experts, ids_ref, levels_ref, *refs):
    *piece_refs, mixed_ref = refs
    count = mixed_ref.shape[0]
    expert = lax.axis_index("grp") // 2
    row = lax.broadcasted_iota(jnp.int32, (count, count), 0)
    column = lax.broadcasted_iota(jnp.int32, (count, count), 1)
    ids = ids_ref[...]
    levels = levels_ref[...].astype(jnp.float32)
    whole = jnp.sum(levels, axis=0, keepdims=True)
    mixed = jnp.zeros(mixed_ref.shape, jnp.float32)
    for s in range(experts):
        source = lax.rem(expert - s + experts, experts)
        weight = ROUTED_SCALE * jnp.sum(jnp.where(ids == source, levels, 0.0), axis=0, keepdims=True) / whole
        upright = jnp.sum(jnp.where(row == column, weight, 0.0), axis=1, keepdims=True)
        total = piece_refs[s * n_tp][...].astype(jnp.float32)
        for t in range(1, n_tp):
            total = total + piece_refs[s * n_tp + t][...].astype(jnp.float32)
        mixed = mixed + upright * total.astype(jnp.bfloat16).astype(jnp.float32)
    mixed_ref[...] = mixed.astype(mixed_ref.dtype)


def mix(expert_ids, gate_levels, pieces, n_tp, experts):
    return pl.pallas_call(
        functools.partial(mix_kernel, n_tp, experts),
        out_shape=jax.ShapeDtypeStruct(pieces[0].shape, jnp.bfloat16),
        compiler_params=pltpu.CompilerParams(vmem_limit_bytes=12 * MIB),
    )(expert_ids.T, gate_levels.T, *pieces)


def per_device(tokens, expert_ids, gate_levels, gate_weight, up_weight, down_weight):
    bf16, f32 = jnp.bfloat16, jnp.float32
    experts = lax.axis_size("grp") // 2
    n_tp, n_ex = lax.axis_size("tp"), lax.axis_size("ex")
    count, width = tokens.shape
    w_gate, w_up, w_down = gate_weight[0], up_weight[0], down_weight[0]
    inner = w_down.shape[0]

    def partial_sums(rows):
        parts = [jnp.dot(rows, w, preferred_element_type=f32) for w in (w_gate, w_up)]
        part = jnp.concatenate(parts, axis=1)
        sent = part.astype(bf16)
        return part, sent, [rotate(sent, "ex", s) for s in range(1, n_ex)]

    def partial_out(part, others, paired, kept_flops, part_flops=0):
        if part_flops:
            part = after(part, flops=part_flops)
        for other in others:
            part = part + other.astype(f32)
        hidden = (jax.nn.silu(part[:, :inner]) * part[:, inner:]).astype(bf16)
        out = jnp.dot(hidden, w_down, preferred_element_type=f32)
        kept, sent = jnp.split(out, 2, axis=0)
        if paired:
            own, other = kept.reshape(n_tp, count, width), sent.reshape(n_tp, count, width)
            kept = [own[places.index(t)] for t in (0, half)]
            sent = [other[places.index(t)] for t in (0, half)]
            for t in range(1, half):
                low, high = places.index(t), places.index(n_tp - t)
                for mine, theirs in ((own, other), (other, own)):
                    kept.append(jnp.where(odd, mine[high], mine[low]))
                    sent.append(jnp.where(odd, theirs[low], theirs[high]))
            kept, sent = jnp.concatenate(kept, axis=0), jnp.concatenate(sent, axis=0)
        swapped = swap_half(sent.astype(bf16)).astype(f32)
        if kept_flops:
            kept = after(kept, flops=kept_flops)
        return kept + swapped

    half = n_tp // 2
    odd = lax.axis_index("grp") % 2 == 1
    places = tuple(range(n_tp))
    held = copied(tokens)
    blocks = [held] + [exchange(tokens, 0, t) for t in places[1:]]
    far = [[rotate_experts(rows, s) for rows in blocks] for s in range(1, experts)]
    near = jnp.concatenate(blocks, axis=0)
    near_swapped = swap_half(after(near, *(line[1] for line in far)))
    near = jnp.concatenate([near, near_swapped], axis=0)
    near_part, near_sent, near_others = partial_sums(near)
    far = [after(rows, near_sent) if i == n_tp - 1 else rows for line in far for i, rows in enumerate(line)]
    far = jnp.concatenate(far, axis=0)
    far_swapped = swap_half(far)
    far = jnp.concatenate([after(far, flops=3450000000), far_swapped], axis=0)
    far_part, far_sent, far_others = partial_sums(far)
    near_out = partial_out(near_part, [after(other, far_sent) for other in near_others], True, 3450000000, 0)
    near_sent = near_out[count:].astype(bf16)
    middle = exchange(near_sent[:count], 0, -half)
    pairs = [exchange(near_sent[(2 * i - 1) * count : (2 * i + 1) * count], 0, -i, i - n_tp) for i in range(1, half)]
    far_out = partial_out(far_part, [after(other, near_out) for other in far_others], False, 0, 0)
    far_out = far_out.reshape(experts - 1, n_tp, count, width).astype(bf16)
    far_back = []
    for s in range(1, experts):
        far_back += [exchange(far_out[experts - 1 - s, i], s, -t) for i, t in enumerate(places)]
    pairs = [after(pair, far_back[n_tp - 1]) for pair in pairs]
    handed = swap_half(jnp.concatenate([pair[count:] for pair in pairs], axis=0))
    pieces = [near_out[:count], middle]
    for i, pair in enumerate(pairs):
        pieces += [pair[:count], handed[i * count : (i + 1) * count]]
    pieces += far_back
    return mix(expert_ids, gate_levels, pieces, n_tp, experts)


def solution(mesh):
    return jax.shard_map(
        per_device,
        mesh=mesh,
        in_specs=(
            P(("grp", "tp"), "ex"),
            P(("grp", "tp"), None),
            P(("grp", "tp"), None),
            P("grp", "ex", "tp"),
            P("grp", "ex", "tp"),
            P("grp", "tp", "ex"),
        ),
        out_specs=P(("grp", "tp"), "ex"),
        check_vma=False,
    )
```

```python
import functools

import jax
import jax.numpy as jnp
from jax import lax
from jax.experimental import pallas as pl
from jax.experimental.pallas import tpu as pltpu
from jax.sharding import PartitionSpec as P

ROUTED_SCALE = 2.5
MIB = 1024 * 1024


def rotate(value, axis, by):
    size = lax.axis_size(axis)
    return lax.ppermute(value, axis, [(i, (i + by) % size) for i in range(size)])


def rotate_experts(value, by):
    groups = lax.axis_size("grp")
    return lax.ppermute(value, "grp", [(i, (i + 2 * by) % groups) for i in range(groups)])


def partner(place, step, size):
    return place ^ abs(step) if size & (size - 1) == 0 else (place + step) % size


def exchange(value, by_expert, *steps):
    groups, n_tp = lax.axis_size("grp"), lax.axis_size("tp")
    pairs = []
    for g in range(groups):
        for t in range(n_tp):
            to = (g + 2 * by_expert) % groups * n_tp + partner(t, steps[g % len(steps)], n_tp)
            pairs.append((g * n_tp + t, to))
    return lax.ppermute(value, ("grp", "tp"), pairs)


def swap_half(value):
    return lax.ppermute(value, "grp", [(i, i ^ 1) for i in range(lax.axis_size("grp"))])


def hand_on(*refs):
    del refs


def after(value, *earlier, flops=0):
    return pl.pallas_call(
        hand_on,
        out_shape=jax.ShapeDtypeStruct(value.shape, value.dtype),
        in_specs=[pl.BlockSpec(memory_space=pl.ANY)] * (1 + len(earlier)),
        out_specs=pl.BlockSpec(memory_space=pl.ANY),
        input_output_aliases={0: 0},
        cost_estimate=pl.CostEstimate(flops=flops, bytes_accessed=0, transcendentals=0),
        compiler_params=pltpu.CompilerParams(vmem_limit_bytes=MIB),
    )(value, *earlier)


def copy_kernel(from_ref, to_ref):
    to_ref[...] = from_ref[...]


def copied(value):
    return pl.pallas_call(
        copy_kernel,
        out_shape=jax.ShapeDtypeStruct(value.shape, value.dtype),
        compiler_params=pltpu.CompilerParams(vmem_limit_bytes=2 * MIB),
    )(value)


def mix_kernel(n_tp, experts, ids_ref, levels_ref, *refs):
    *piece_refs, mixed_ref = refs
    count = mixed_ref.shape[0]
    expert = lax.axis_index("grp") // 2
    row = lax.broadcasted_iota(jnp.int32, (count, count), 0)
    column = lax.broadcasted_iota(jnp.int32, (count, count), 1)
    ids = ids_ref[...]
    levels = levels_ref[...].astype(jnp.float32)
    whole = jnp.sum(levels, axis=0, keepdims=True)
    mixed = jnp.zeros(mixed_ref.shape, jnp.float32)
    for s in range(experts):
        source = lax.rem(expert - s + experts, experts)
        weight = ROUTED_SCALE * jnp.sum(jnp.where(ids == source, levels, 0.0), axis=0, keepdims=True) / whole
        upright = jnp.sum(jnp.where(row == column, weight, 0.0), axis=1, keepdims=True)
        total = piece_refs[s * n_tp][...].astype(jnp.float32)
        for t in range(1, n_tp):
            total = total + piece_refs[s * n_tp + t][...].astype(jnp.float32)
        mixed = mixed + upright * total.astype(jnp.bfloat16).astype(jnp.float32)
    mixed_ref[...] = mixed.astype(mixed_ref.dtype)


def mix(expert_ids, gate_levels, pieces, n_tp, experts):
    return pl.pallas_call(
        functools.partial(mix_kernel, n_tp, experts),
        out_shape=jax.ShapeDtypeStruct(pieces[0].shape, jnp.bfloat16),
        compiler_params=pltpu.CompilerParams(vmem_limit_bytes=12 * MIB),
    )(expert_ids.T, gate_levels.T, *pieces)


def per_device(tokens, expert_ids, gate_levels, gate_weight, up_weight, down_weight):
    bf16, f32 = jnp.bfloat16, jnp.float32
    experts = lax.axis_size("grp") // 2
    n_tp, n_ex = lax.axis_size("tp"), lax.axis_size("ex")
    count, width = tokens.shape
    w_gate, w_up, w_down = gate_weight[0], up_weight[0], down_weight[0]
    inner = w_down.shape[0]

    def partial_sums(rows):
        parts = [jnp.dot(rows, w, preferred_element_type=f32) for w in (w_gate, w_up)]
        part = jnp.concatenate(parts, axis=1)
        sent = part.astype(bf16)
        return part, sent, [rotate(sent, "ex", s) for s in range(1, n_ex)]

    def partial_out(part, others, paired, kept_flops, part_flops=0):
        if part_flops:
            part = after(part, flops=part_flops)
        for other in others:
            part = part + other.astype(f32)
        hidden = (jax.nn.silu(part[:, :inner]) * part[:, inner:]).astype(bf16)
        out = jnp.dot(hidden, w_down, preferred_element_type=f32)
        kept, sent = jnp.split(out, 2, axis=0)
        if paired:
            own, other = kept.reshape(n_tp, count, width), sent.reshape(n_tp, count, width)
            kept = [own[places.index(t)] for t in (0, half)]
            sent = [other[places.index(t)] for t in (0, half)]
            for t in range(1, half):
                low, high = places.index(t), places.index(n_tp - t)
                for mine, theirs in ((own, other), (other, own)):
                    kept.append(jnp.where(odd, mine[high], mine[low]))
                    sent.append(jnp.where(odd, theirs[low], theirs[high]))
            kept, sent = jnp.concatenate(kept, axis=0), jnp.concatenate(sent, axis=0)
        swapped = swap_half(sent.astype(bf16)).astype(f32)
        if kept_flops:
            kept = after(kept, flops=kept_flops)
        return kept + swapped

    half = n_tp // 2
    odd = lax.axis_index("grp") % 2 == 1
    places = tuple(range(n_tp))
    held = copied(tokens)
    blocks = [held] + [exchange(tokens, 0, t) for t in places[1:]]
    far = [[rotate_experts(rows, s) for rows in blocks] for s in range(1, experts)]
    near = jnp.concatenate(blocks, axis=0)
    near_swapped = swap_half(after(near, *(line[1] for line in far)))
    near = jnp.concatenate([near, near_swapped], axis=0)
    near_part, near_sent, near_others = partial_sums(near)
    far = [after(rows, near_sent) if i == n_tp - 1 else rows for line in far for i, rows in enumerate(line)]
    far = jnp.concatenate(far, axis=0)
    far_swapped = swap_half(far)
    far = jnp.concatenate([after(far, flops=1725000000), far_swapped], axis=0)
    far_part, far_sent, far_others = partial_sums(far)
    near_out = partial_out(near_part, [after(other, far_sent) for other in near_others], True, 1725000000, 0)
    near_sent = near_out[count:].astype(bf16)
    middle = exchange(near_sent[:count], 0, -half)
    pairs = [exchange(near_sent[(2 * i - 1) * count : (2 * i + 1) * count], 0, -i, i - n_tp) for i in range(1, half)]
    far_out = partial_out(far_part, [after(other, near_out) for other in far_others], False, 0, 0)
    far_out = far_out.reshape(experts - 1, n_tp, count, width).astype(bf16)
    far_back = []
    for s in range(1, experts):
        far_back += [exchange(far_out[experts - 1 - s, i], s, -t) for i, t in enumerate(places)]
    pairs = [after(pair, far_back[n_tp - 1]) for pair in pairs]
    handed = swap_half(jnp.concatenate([pair[count:] for pair in pairs], axis=0))
    pieces = [near_out[:count], middle]
    for i, pair in enumerate(pairs):
        pieces += [pair[:count], handed[i * count : (i + 1) * count]]
    pieces += far_back
    return mix(expert_ids, gate_levels, pieces, n_tp, experts)


def solution(mesh):
    return jax.shard_map(
        per_device,
        mesh=mesh,
        in_specs=(
            P(("grp", "tp"), "ex"),
            P(("grp", "tp"), None),
            P(("grp", "tp"), None),
            P("grp", "ex", "tp"),
            P("grp", "ex", "tp"),
            P("grp", "tp", "ex"),
        ),
        out_specs=P(("grp", "tp"), "ex"),
        check_vma=False,
    )
```

```python
import functools

import jax
import jax.numpy as jnp
from jax import lax
from jax.experimental import pallas as pl
from jax.experimental.pallas import tpu as pltpu
from jax.sharding import PartitionSpec as P

ROUTED_SCALE = 2.5
MIB = 1024 * 1024


def rotate(value, axis, by):
    size = lax.axis_size(axis)
    return lax.ppermute(value, axis, [(i, (i + by) % size) for i in range(size)])


def rotate_experts(value, by):
    groups = lax.axis_size("grp")
    return lax.ppermute(value, "grp", [(i, (i + 2 * by) % groups) for i in range(groups)])


def partner(place, step, size):
    return place ^ abs(step) if size & (size - 1) == 0 else (place + step) % size


def exchange(value, by_expert, step):
    groups, n_tp = lax.axis_size("grp"), lax.axis_size("tp")
    pairs = []
    for g in range(groups):
        for t in range(n_tp):
            to = (g + 2 * by_expert) % groups * n_tp + partner(t, step, n_tp)
            pairs.append((g * n_tp + t, to))
    return lax.ppermute(value, ("grp", "tp"), pairs)


def swap_half(value):
    return lax.ppermute(value, "grp", [(i, i ^ 1) for i in range(lax.axis_size("grp"))])


def hand_on(*refs):
    del refs


def after(value, *earlier, flops=0):
    return pl.pallas_call(
        hand_on,
        out_shape=jax.ShapeDtypeStruct(value.shape, value.dtype),
        in_specs=[pl.BlockSpec(memory_space=pl.ANY)] * (1 + len(earlier)),
        out_specs=pl.BlockSpec(memory_space=pl.ANY),
        input_output_aliases={0: 0},
        cost_estimate=pl.CostEstimate(flops=flops, bytes_accessed=0, transcendentals=0),
        compiler_params=pltpu.CompilerParams(vmem_limit_bytes=MIB),
    )(value, *earlier)


def copy_kernel(from_ref, to_ref):
    to_ref[...] = from_ref[...]


def copied(value):
    return pl.pallas_call(
        copy_kernel,
        out_shape=jax.ShapeDtypeStruct(value.shape, value.dtype),
        compiler_params=pltpu.CompilerParams(vmem_limit_bytes=2 * MIB),
    )(value)


def mix_kernel(n_tp, experts, ids_ref, levels_ref, *refs):
    *piece_refs, mixed_ref = refs
    count = mixed_ref.shape[0]
    expert = lax.axis_index("grp") // 2
    row = lax.broadcasted_iota(jnp.int32, (count, count), 0)
    column = lax.broadcasted_iota(jnp.int32, (count, count), 1)
    ids = ids_ref[...]
    levels = levels_ref[...].astype(jnp.float32)
    whole = jnp.sum(levels, axis=0, keepdims=True)
    mixed = jnp.zeros(mixed_ref.shape, jnp.float32)
    for s in range(experts):
        source = lax.rem(expert - s + experts, experts)
        weight = ROUTED_SCALE * jnp.sum(jnp.where(ids == source, levels, 0.0), axis=0, keepdims=True) / whole
        upright = jnp.sum(jnp.where(row == column, weight, 0.0), axis=1, keepdims=True)
        total = piece_refs[s * n_tp][...].astype(jnp.float32)
        for t in range(1, n_tp):
            total = total + piece_refs[s * n_tp + t][...].astype(jnp.float32)
        mixed = mixed + upright * total.astype(jnp.bfloat16).astype(jnp.float32)
    mixed_ref[...] = mixed.astype(mixed_ref.dtype)


def mix(expert_ids, gate_levels, pieces, n_tp, experts):
    return pl.pallas_call(
        functools.partial(mix_kernel, n_tp, experts),
        out_shape=jax.ShapeDtypeStruct(pieces[0].shape, jnp.bfloat16),
        compiler_params=pltpu.CompilerParams(vmem_limit_bytes=12 * MIB),
    )(expert_ids.T, gate_levels.T, *pieces)


def per_device(tokens, expert_ids, gate_levels, gate_weight, up_weight, down_weight):
    bf16, f32 = jnp.bfloat16, jnp.float32
    experts = lax.axis_size("grp") // 2
    n_tp, n_ex = lax.axis_size("tp"), lax.axis_size("ex")
    count, width = tokens.shape
    w_gate, w_up, w_down = gate_weight[0], up_weight[0], down_weight[0]
    inner = w_down.shape[0]

    def partial_sums(rows):
        parts = [jnp.dot(rows, w, preferred_element_type=f32) for w in (w_gate, w_up)]
        part = jnp.concatenate(parts, axis=1)
        sent = part.astype(bf16)
        return part, sent, [rotate(sent, "ex", s) for s in range(1, n_ex)]

    def partial_out(part, others, kept_flops, part_flops=0, *earlier):
        if part_flops:
            part = after(part, flops=part_flops)
        for other in others:
            part = part + other.astype(f32)
        hidden = (jax.nn.silu(part[:, :inner]) * part[:, inner:]).astype(bf16)
        out = jnp.dot(hidden, w_down, preferred_element_type=f32)
        kept = out.shape[0] // 2
        swapped = swap_half(out[kept:].astype(bf16)).astype(f32)
        if kept_flops:
            out = after(after(out, *earlier) if earlier else out, flops=kept_flops)
        return out[:kept] + swapped

    held = copied(tokens)
    places = (0, 1, *range(n_tp - 1, 1, -1))
    blocks = [held] + [exchange(tokens, 0, t) for t in places[1:]]
    far = [[rotate_experts(rows, s) for rows in blocks] for s in range(1, experts)]
    near = jnp.concatenate(blocks, axis=0)
    near_swapped = swap_half(after(near, *(line[1] for line in far)))
    near = jnp.concatenate([near, near_swapped], axis=0)
    near_part, near_sent, near_others = partial_sums(near)
    far = [after(rows, near_sent) if i == n_tp - 1 else rows for line in far for i, rows in enumerate(line)]
    far = jnp.concatenate(far, axis=0)
    far_swapped = swap_half(far)
    far = jnp.concatenate([after(far, flops=3450000000), far_swapped], axis=0)
    far_part, far_sent, far_others = partial_sums(far)
    near_out = partial_out(near_part, [after(other, far_sent) for other in near_others], 3450000000, 0)
    near_out = near_out.reshape(n_tp, count, width)
    near_sent = near_out[1:].astype(bf16)
    pieces = [near_out[0]] + [exchange(near_sent[i], 0, -t) for i, t in enumerate(places[1:])]
    far_out = partial_out(far_part, [after(other, near_sent) for other in far_others], 0, 0)
    far_out = far_out.reshape(experts - 1, n_tp, count, width).astype(bf16)
    for s in range(1, experts):
        pieces += [exchange(far_out[experts - 1 - s, i], s, -t) for i, t in enumerate(places)]
    return mix(expert_ids, gate_levels, pieces, n_tp, experts)


def solution(mesh):
    return jax.shard_map(
        per_device,
        mesh=mesh,
        in_specs=(
            P(("grp", "tp"), "ex"),
            P(("grp", "tp"), None),
            P(("grp", "tp"), None),
            P("grp", "ex", "tp"),
            P("grp", "ex", "tp"),
            P("grp", "tp", "ex"),
        ),
        out_specs=P(("grp", "tp"), "ex"),
        check_vma=False,
    )
```

```python
import functools

import jax
import jax.numpy as jnp
from jax import lax
from jax.experimental import pallas as pl
from jax.experimental.pallas import tpu as pltpu
from jax.sharding import PartitionSpec as P

ROUTED_SCALE = 2.5
MIB = 1024 * 1024


def rotate(value, axis, by):
    size = lax.axis_size(axis)
    return lax.ppermute(value, axis, [(i, (i + by) % size) for i in range(size)])


def rotate_experts(value, by):
    groups = lax.axis_size("grp")
    return lax.ppermute(value, "grp", [(i, (i + 2 * by) % groups) for i in range(groups)])


def partner(place, step, size):
    return place ^ abs(step) if size & (size - 1) == 0 else (place + step) % size


def exchange(value, by_expert, step):
    groups, n_tp = lax.axis_size("grp"), lax.axis_size("tp")
    pairs = []
    for g in range(groups):
        for t in range(n_tp):
            to = (g + 2 * by_expert) % groups * n_tp + partner(t, step, n_tp)
            pairs.append((g * n_tp + t, to))
    return lax.ppermute(value, ("grp", "tp"), pairs)


def swap_half(value):
    return lax.ppermute(value, "grp", [(i, i ^ 1) for i in range(lax.axis_size("grp"))])


def hand_on(*refs):
    del refs


def after(value, *earlier, flops=0):
    return pl.pallas_call(
        hand_on,
        out_shape=jax.ShapeDtypeStruct(value.shape, value.dtype),
        in_specs=[pl.BlockSpec(memory_space=pl.ANY)] * (1 + len(earlier)),
        out_specs=pl.BlockSpec(memory_space=pl.ANY),
        input_output_aliases={0: 0},
        cost_estimate=pl.CostEstimate(flops=flops, bytes_accessed=0, transcendentals=0),
        compiler_params=pltpu.CompilerParams(vmem_limit_bytes=MIB),
    )(value, *earlier)


def copy_kernel(from_ref, to_ref):
    to_ref[...] = from_ref[...]


def copied(value):
    return pl.pallas_call(
        copy_kernel,
        out_shape=jax.ShapeDtypeStruct(value.shape, value.dtype),
        compiler_params=pltpu.CompilerParams(vmem_limit_bytes=2 * MIB),
    )(value)


def mix_kernel(n_tp, experts, ids_ref, levels_ref, *refs):
    *piece_refs, mixed_ref = refs
    count = mixed_ref.shape[0]
    expert = lax.axis_index("grp") // 2
    row = lax.broadcasted_iota(jnp.int32, (count, count), 0)
    column = lax.broadcasted_iota(jnp.int32, (count, count), 1)
    ids = ids_ref[...]
    levels = levels_ref[...].astype(jnp.float32)
    whole = jnp.sum(levels, axis=0, keepdims=True)
    mixed = jnp.zeros(mixed_ref.shape, jnp.float32)
    for s in range(experts):
        source = lax.rem(expert - s + experts, experts)
        weight = ROUTED_SCALE * jnp.sum(jnp.where(ids == source, levels, 0.0), axis=0, keepdims=True) / whole
        upright = jnp.sum(jnp.where(row == column, weight, 0.0), axis=1, keepdims=True)
        total = piece_refs[s * n_tp][...].astype(jnp.float32)
        for t in range(1, n_tp):
            total = total + piece_refs[s * n_tp + t][...].astype(jnp.float32)
        mixed = mixed + upright * total.astype(jnp.bfloat16).astype(jnp.float32)
    mixed_ref[...] = mixed.astype(mixed_ref.dtype)


def mix(expert_ids, gate_levels, pieces, n_tp, experts):
    return pl.pallas_call(
        functools.partial(mix_kernel, n_tp, experts),
        out_shape=jax.ShapeDtypeStruct(pieces[0].shape, jnp.bfloat16),
        compiler_params=pltpu.CompilerParams(vmem_limit_bytes=12 * MIB),
    )(expert_ids.T, gate_levels.T, *pieces)


def per_device(tokens, expert_ids, gate_levels, gate_weight, up_weight, down_weight):
    bf16, f32 = jnp.bfloat16, jnp.float32
    experts = lax.axis_size("grp") // 2
    n_tp, n_ex = lax.axis_size("tp"), lax.axis_size("ex")
    count, width = tokens.shape
    w_gate, w_up, w_down = gate_weight[0], up_weight[0], down_weight[0]
    inner = w_down.shape[0]

    def partial_sums(rows):
        parts = [jnp.dot(rows, w, preferred_element_type=f32) for w in (w_gate, w_up)]
        part = jnp.concatenate(parts, axis=1)
        sent = part.astype(bf16)
        return part, sent, [rotate(sent, "ex", s) for s in range(1, n_ex)]

    def partial_out(part, others, kept_flops, part_flops=0, *earlier):
        if part_flops:
            part = after(part, flops=part_flops)
        for other in others:
            part = part + other.astype(f32)
        hidden = (jax.nn.silu(part[:, :inner]) * part[:, inner:]).astype(bf16)
        out = jnp.dot(hidden, w_down, preferred_element_type=f32)
        kept = out.shape[0] // 2
        swapped = swap_half(out[kept:].astype(bf16)).astype(f32)
        if kept_flops:
            out = after(after(out, *earlier) if earlier else out, flops=kept_flops)
        return out[:kept] + swapped

    held = copied(tokens)
    places = tuple(range(n_tp))
    blocks = [held] + [exchange(tokens, 0, t) for t in places[1:]]
    far = [[rotate_experts(rows, s) for rows in (tokens, *blocks[1:])] for s in range(1, experts)]
    near = jnp.concatenate(blocks, axis=0)
    near_swapped = swap_half(after(near, *(line[1] for line in far)))
    near = jnp.concatenate([near, near_swapped], axis=0)
    near_part, near_sent, near_others = partial_sums(near)
    far = [after(rows, near_sent) if i == n_tp - 1 else rows for line in far for i, rows in enumerate(line)]
    far = jnp.concatenate(far, axis=0)
    far_swapped = swap_half(far)
    far = jnp.concatenate([after(far, flops=3450000000), far_swapped], axis=0)
    far_part, far_sent, far_others = partial_sums(far)
    near_out = partial_out(near_part, [after(other, far_sent) for other in near_others], 3450000000, 0)
    near_out = near_out.reshape(n_tp, count, width)
    near_sent = near_out[1:].astype(bf16)
    pieces = [near_out[0]] + [exchange(near_sent[i], 0, -t) for i, t in enumerate(places[1:])]
    far_out = partial_out(far_part, [after(other, near_sent) for other in far_others], 0, 0)
    far_out = far_out.reshape(experts - 1, n_tp, count, width).astype(bf16)
    for s in range(1, experts):
        pieces += [exchange(far_out[experts - 1 - s, i], s, -t) for i, t in enumerate(places)]
    return mix(expert_ids, gate_levels, pieces, n_tp, experts)


def solution(mesh):
    return jax.shard_map(
        per_device,
        mesh=mesh,
        in_specs=(
            P(("grp", "tp"), "ex"),
            P(("grp", "tp"), None),
            P(("grp", "tp"), None),
            P("grp", "ex", "tp"),
            P("grp", "ex", "tp"),
            P("grp", "tp", "ex"),
        ),
        out_specs=P(("grp", "tp"), "ex"),
        check_vma=False,
    )
```

```python
import functools

import jax
import jax.numpy as jnp
from jax import lax
from jax.experimental import pallas as pl
from jax.experimental.pallas import tpu as pltpu
from jax.sharding import PartitionSpec as P

ROUTED_SCALE = 2.5
MIB = 1024 * 1024


def rotate(value, axis, by):
    size = lax.axis_size(axis)
    return lax.ppermute(value, axis, [(i, (i + by) % size) for i in range(size)])


def rotate_experts(value, by):
    groups = lax.axis_size("grp")
    return lax.ppermute(value, "grp", [(i, (i + 2 * by) % groups) for i in range(groups)])


def partner(place, step, size):
    return place ^ abs(step) if size & (size - 1) == 0 else (place + step) % size


def exchange(value, by_expert, step):
    groups, n_tp = lax.axis_size("grp"), lax.axis_size("tp")
    pairs = []
    for g in range(groups):
        for t in range(n_tp):
            to = (g + 2 * by_expert) % groups * n_tp + partner(t, step, n_tp)
            pairs.append((g * n_tp + t, to))
    return lax.ppermute(value, ("grp", "tp"), pairs)


def swap_half(value):
    return lax.ppermute(value, "grp", [(i, i ^ 1) for i in range(lax.axis_size("grp"))])


def hand_on(*refs):
    del refs


def after(value, *earlier, flops=0):
    return pl.pallas_call(
        hand_on,
        out_shape=jax.ShapeDtypeStruct(value.shape, value.dtype),
        in_specs=[pl.BlockSpec(memory_space=pl.ANY)] * (1 + len(earlier)),
        out_specs=pl.BlockSpec(memory_space=pl.ANY),
        input_output_aliases={0: 0},
        cost_estimate=pl.CostEstimate(flops=flops, bytes_accessed=0, transcendentals=0),
        compiler_params=pltpu.CompilerParams(vmem_limit_bytes=MIB),
    )(value, *earlier)


def copy_kernel(from_ref, to_ref):
    to_ref[...] = from_ref[...]


def copied(value):
    return pl.pallas_call(
        copy_kernel,
        out_shape=jax.ShapeDtypeStruct(value.shape, value.dtype),
        compiler_params=pltpu.CompilerParams(vmem_limit_bytes=2 * MIB),
    )(value)


def mix_kernel(n_tp, experts, ids_ref, levels_ref, *refs):
    *piece_refs, mixed_ref = refs
    count = mixed_ref.shape[0]
    expert = lax.axis_index("grp") // 2
    row = lax.broadcasted_iota(jnp.int32, (count, count), 0)
    column = lax.broadcasted_iota(jnp.int32, (count, count), 1)
    ids = ids_ref[...]
    levels = levels_ref[...].astype(jnp.float32)
    whole = jnp.sum(levels, axis=0, keepdims=True)
    mixed = jnp.zeros(mixed_ref.shape, jnp.float32)
    for s in range(experts):
        source = lax.rem(expert - s + experts, experts)
        weight = ROUTED_SCALE * jnp.sum(jnp.where(ids == source, levels, 0.0), axis=0, keepdims=True) / whole
        upright = jnp.sum(jnp.where(row == column, weight, 0.0), axis=1, keepdims=True)
        total = piece_refs[s * n_tp][...].astype(jnp.float32)
        for t in range(1, n_tp):
            total = total + piece_refs[s * n_tp + t][...].astype(jnp.float32)
        mixed = mixed + upright * total.astype(jnp.bfloat16).astype(jnp.float32)
    mixed_ref[...] = mixed.astype(mixed_ref.dtype)


def mix(expert_ids, gate_levels, pieces, n_tp, experts):
    return pl.pallas_call(
        functools.partial(mix_kernel, n_tp, experts),
        out_shape=jax.ShapeDtypeStruct(pieces[0].shape, jnp.bfloat16),
        compiler_params=pltpu.CompilerParams(vmem_limit_bytes=12 * MIB),
    )(expert_ids.T, gate_levels.T, *pieces)


def per_device(tokens, expert_ids, gate_levels, gate_weight, up_weight, down_weight):
    bf16, f32 = jnp.bfloat16, jnp.float32
    experts = lax.axis_size("grp") // 2
    n_tp, n_ex = lax.axis_size("tp"), lax.axis_size("ex")
    count, width = tokens.shape
    w_gate, w_up, w_down = gate_weight[0], up_weight[0], down_weight[0]
    inner = w_down.shape[0]

    def partial_sums(rows):
        parts = [jnp.dot(rows, w, preferred_element_type=f32) for w in (w_gate, w_up)]
        part = jnp.concatenate(parts, axis=1)
        sent = part.astype(bf16)
        return part, sent, [rotate(sent, "ex", s) for s in range(1, n_ex)]

    def partial_out(part, others, kept_flops, part_flops=0, *earlier):
        if part_flops:
            part = after(part, flops=part_flops)
        for other in others:
            part = part + other.astype(f32)
        hidden = (jax.nn.silu(part[:, :inner]) * part[:, inner:]).astype(bf16)
        out = jnp.dot(hidden, w_down, preferred_element_type=f32)
        kept = out.shape[0] // 2
        swapped = swap_half(out[kept:].astype(bf16)).astype(f32)
        if kept_flops:
            out = after(after(out, *earlier) if earlier else out, flops=kept_flops)
        return out[:kept] + swapped

    held = copied(tokens)
    places = (0, n_tp - 1, *range(1, n_tp - 1))
    blocks = [held] + [exchange(tokens, 0, t) for t in places[1:]]
    far = [[rotate_experts(rows, s) for rows in (tokens, *blocks[1:])] for s in range(1, experts)]
    near = jnp.concatenate(blocks, axis=0)
    near_swapped = swap_half(after(near, *(line[places.index(1)] for line in far)))
    near = jnp.concatenate([near, near_swapped], axis=0)
    near_part, near_sent, near_others = partial_sums(near)
    far = [after(rows, near_sent) if i == n_tp - 1 else rows for line in far for i, rows in enumerate(line)]
    far = jnp.concatenate(far, axis=0)
    far_swapped = swap_half(far)
    far = jnp.concatenate([after(far, flops=3450000000), far_swapped], axis=0)
    far_part, far_sent, far_others = partial_sums(far)
    near_out = partial_out(near_part, [after(other, far_sent) for other in near_others], 3450000000, 0)
    near_out = near_out.reshape(n_tp, count, width)
    near_sent = near_out[1:].astype(bf16)
    pieces = [near_out[0]] + [exchange(near_sent[i], 0, -t) for i, t in enumerate(places[1:])]
    far_out = partial_out(far_part, [after(other, near_sent) for other in far_others], 0, 0)
    far_out = far_out.reshape(experts - 1, n_tp, count, width).astype(bf16)
    for s in range(1, experts):
        pieces += [exchange(far_out[experts - 1 - s, i], s, -t) for i, t in enumerate(places)]
    return mix(expert_ids, gate_levels, pieces, n_tp, experts)


def solution(mesh):
    return jax.shard_map(
        per_device,
        mesh=mesh,
        in_specs=(
            P(("grp", "tp"), "ex"),
            P(("grp", "tp"), None),
            P(("grp", "tp"), None),
            P("grp", "ex", "tp"),
            P("grp", "ex", "tp"),
            P("grp", "tp", "ex"),
        ),
        out_specs=P(("grp", "tp"), "ex"),
        check_vma=False,
    )
```
